512 devices in a mesh: tile: 64 (over x, y, core), fblk: 8 (over z).
Axes of the slice: x: 4, y: 8, z: 8, core: 2. Of those that a mesh axis runs over, the one named last changes fastest.
Arguments:
- planes: float32 [512, 1024, 128], P(('fblk', 'tile')), may hold values from -40000 to 40000
- widths: int32 [4], replicated, may hold values from 1 to 8, as said below
Outputs:
- peak_maps: float32 [4, 1024, 128], P(None, 'tile')
The draws below stay inside these ranges and needn't reach their ends.
Inputs may be any that keep to these rules, and one draw needn't show every extreme that they name: `widths`: some kernel has width 8 in every draw.
All inputs are finite; a program needn't handle non-finite values.
Results may differ from the reference program's by a relative error of at most 0.0001.
Values sent between devices are 32-bit elements; how exact they have to be, the bound alone decides.
No kernel may reach another device: no remote copies, remote signals or barrier semaphores. Data moves between devices by JAX's collectives and lax.ppermute only.
A program may use at most 64 MiB of HBM per device.

```python
import jax
import jax.numpy as jnp
from jax import lax

KERNELS = 4
RAD = 8
MAXW = 8
NX = 128
NY = 1024
CHANS = 512


def draw_planes(key, part):
    key = jax.random.fold_in(key, 11)
    key_field, key_channel, key_row, key_column = jax.random.split(key, 4)
    positions = jnp.arange(NY).astype(jnp.float32) / NY
    random_field = jnp.clip(jax.random.normal(key_field, (CHANS, NY, NX), jnp.float32), -4.0, 4.0)
    rising = 3.0 ** positions
    channel_scale = 10.0 ** jax.random.uniform(key_channel, (CHANS,), jnp.float32)
    row_scale = rising * 10.0 ** jax.random.uniform(key_row, (NY,), jnp.float32)
    column_scale = 10.0 ** jax.random.uniform(key_column, (NX,), jnp.float32)
    return random_field * channel_scale[:, None, None] * row_scale[None, :, None] * column_scale[None, None, :]


def draw_widths(key, part):
    key = jax.random.fold_in(key, 23)
    key_values, key_pick = jax.random.split(key)
    values = jax.random.randint(key_values, (KERNELS,), 1, MAXW + 1)
    chosen = jax.random.randint(key_pick, (), 0, KERNELS)
    return jnp.where(jnp.arange(KERNELS) == chosen, MAXW, values).astype(jnp.int32)


def setup_inputs(seed: int = 0) -> dict:
    streams_of = jax.random.split(jax.random.key(seed), 3)
    return {
        "planes": draw_planes(jax.random.fold_in(streams_of[2], 71), 0),
        "widths": draw_widths(jax.random.fold_in(streams_of[2], 71), 0),
    }


SIGMAS = (1.0, 1.6, 2.3, 3.2)
EPSILON = 1e-06

def kernel_for(sigma):
    offsets = jnp.arange(2 * RAD + 1).astype(jnp.float32) - RAD
    values = jnp.exp(-offsets * offsets / (2.0 * sigma * sigma))
    return values / jnp.sum(values)

def pad_along(values, along):
    margins = [(0, 0)] * values.ndim
    margins[along] = (RAD, RAD)
    return jnp.pad(values, margins)

def filter_along(padded, kernel, along):
    length = padded.shape[along] - 2 * RAD
    summed = jnp.zeros(lax.slice_in_dim(padded, 0, length, axis=along).shape, jnp.float32)
    for offset in range(2 * RAD + 1):
        summed = summed + kernel[offset] * lax.slice_in_dim(padded, offset, offset + length, axis=along)
    return summed

def boxcar(extended, width, channels):
    scale = 1.0 / jnp.sqrt(width.astype(jnp.float32))
    summed = jnp.zeros((channels,) + extended.shape[1:], jnp.float32)
    for offset in range(MAXW):
        weight = jnp.where(offset < width, 1.0, 0.0).astype(jnp.float32) * scale
        summed = summed + weight * extended[offset:offset + channels]
    return summed

def reference(planes, widths):
    extended = jnp.pad(planes, ((0, MAXW - 1), (0, 0), (0, 0)))
    peak_list = []
    for kernel_id in range(KERNELS):
        kernel = kernel_for(SIGMAS[kernel_id])
        spectral = boxcar(extended, widths[kernel_id], CHANS)

        def smooth_plane(plane):
            horizontal = filter_along(pad_along(plane, 1), kernel, 1)
            return filter_along(pad_along(horizontal, 0), kernel, 0)
        smoothed = lax.map(smooth_plane, spectral)
        sum_squares = lax.optimization_barrier(jnp.sum(smoothed * smoothed, axis=(1, 2)))
        rms_values = jnp.sqrt(sum_squares / (NY * NX) + EPSILON)
        peak_list.append(lax.optimization_barrier(jnp.max(smoothed / rms_values[:, None, None], axis=0)))
    return jnp.stack(peak_list)
```

```python
import jax
import jax.numpy as jnp
import numpy as np
from jax import lax
from jax.experimental import pallas as pl
from jax.experimental.pallas import tpu as pltpu
from jax.sharding import PartitionSpec as P

KERNELS = 4
RAD = 8
MAXW = 8
SIGMAS = (1.0, 1.6, 2.3, 3.2)
EPSILON = 1e-06
ROWS = 16
SPAN = ROWS + 2 * RAD
GROUP = 8
NX = 128
BF = jnp.bfloat16
F32 = jnp.float32
VMEM = pl.BlockSpec(memory_space=pltpu.VMEM)
SMEM = pl.BlockSpec(memory_space=pltpu.SMEM)
PARAMS = pltpu.CompilerParams(vmem_limit_bytes=32 * 1024 * 1024)


def taps(sigma):
    offsets = np.arange(2 * RAD + 1) - RAD
    values = np.exp(-(offsets**2) / (2.0 * sigma * sigma))
    return values / values.sum()


def split(matrix):
    matrix = np.asarray(matrix, np.float32)
    high = matrix.astype(BF)
    return high, (matrix - high.astype(np.float32)).astype(BF)


def vertical_matrix():
    out = np.zeros((KERNELS, GROUP, ROWS, 2 * GROUP, SPAN))
    for k, sigma in enumerate(SIGMAS):
        weights = taps(sigma)
        for row in range(ROWS):
            for channel in range(GROUP):
                for offset in range(MAXW):
                    out[k, channel, row, channel + offset, row : row + 2 * RAD + 1] = weights
    return out.reshape(KERNELS * GROUP * ROWS, 2 * GROUP * SPAN)


def horizontal_matrices():
    out = np.zeros((KERNELS, 2, NX, 2, NX))
    for k, sigma in enumerate(SIGMAS):
        weights = taps(sigma)
        for x in range(NX):
            for j in range(-RAD, RAD + 1):
                if 0 <= x + j < NX:
                    out[k, :, x + j, :, x] = weights[j + RAD] * np.eye(2)
    return out.reshape(KERNELS, 2 * NX, 2 * NX)


def halves(values):
    high = values.astype(BF)
    return high, (values - high.astype(F32)).astype(BF)


def dot3(a_high, a_low, b_high, b_low):
    def dot(a, b):
        return jnp.dot(a, b, preferred_element_type=F32)

    return dot(a_high, b_high) + (dot(a_low, b_high) + dot(a_high, b_low))


def mask_kernel(widths, high_in, low_in, high, low):
    block = GROUP * ROWS
    shape = (block, 2 * GROUP * SPAN)
    offset = lax.broadcasted_iota(jnp.int32, shape, 1) // SPAN - lax.broadcasted_iota(jnp.int32, shape, 0) // ROWS
    for k in range(KERNELS):
        keep = jnp.where(offset < widths[k], 1.0, 0.0)
        rows = pl.ds(k * block, block)
        high[rows, :] = (high_in[rows, :].astype(F32) * keep).astype(BF)
        low[rows, :] = (low_in[rows, :].astype(F32) * keep).astype(BF)


def smooth_kernel(own, before, after, edge, a_high, a_low, h_high, h_low, smoothed, sums, x_high, x_low):
    channels = own.shape[0]
    x = jnp.concatenate([before[...], own[...], after[...]], axis=1)
    x_high[0:channels], x_low[0:channels] = halves(x)
    x = jnp.concatenate([edge[...], jnp.zeros((1, SPAN, NX), F32)], axis=0)
    x_high[channels:], x_low[channels:] = halves(x)
    block = GROUP * ROWS
    partial = [[None] * (channels // GROUP) for _ in range(KERNELS)]
    for pair in range(channels // (2 * GROUP)):

        def side_by_side(ref):
            first = 2 * pair * GROUP
            parts = [ref[first + s : first + s + 2 * GROUP].reshape(2 * GROUP * SPAN, NX) for s in (0, GROUP)]
            return jnp.concatenate(parts, axis=1)

        xh, xl = side_by_side(x_high), side_by_side(x_low)
        for k in range(KERNELS):
            rows = pl.ds(k * block, block)
            y = dot3(a_high[rows, :], a_low[rows, :], xh, xl)
            yh, yl = halves(y)
            z = dot3(yh, yl, h_high[k], h_low[k])
            smoothed[k, pair] = z
            squares = jnp.sum((z * z).reshape(GROUP, ROWS, 2 * NX), axis=1)
            partial[k][2 * pair] = squares[:, :NX]
            partial[k][2 * pair + 1] = squares[:, NX:]
    stacked = jnp.concatenate([p for row in partial for p in row], axis=0)
    total = lax.dot_general(
        jnp.ones((8, NX), F32), stacked, (((1,), (1,)), ((), ())), precision=lax.Precision.HIGHEST, preferred_element_type=F32
    )
    odd = lax.broadcasted_iota(jnp.int32, sums.shape, 0) % 2
    both = [jnp.broadcast_to(total[0:1, h * NX : (h + 1) * NX], sums.shape) for h in (0, 1)]
    sums[...] = jnp.where(odd == 0, both[0], both[1])


def peak_kernel(cells, copies, widths, received, smoothed, peaks, scale):
    lane_odd = lax.broadcasted_iota(jnp.int32, (received.shape[0], NX), 0) % 2
    values = received[...]
    per_half = 2 * NX // KERNELS
    for h in (0, 1):
        total = lax.dot_general(
            values,
            jnp.where(lane_odd == h, 1.0, 0.0),
            (((0,), (0,)), ((), ())),
            precision=lax.Precision.HIGHEST,
            preferred_element_type=F32,
        )
        for i in range(KERNELS // 2):
            k = h * (KERNELS // 2) + i
            part = total[i * per_half : (i + 1) * per_half]
            floor = widths[k].astype(F32) * EPSILON
            scale[k] = 1.0 / jnp.sqrt(part * (1.0 / cells) + floor)
    for k in range(KERNELS):
        best = None
        for pair in range(smoothed.shape[1]):
            for g in (0, 1):
                for c in range(GROUP):
                    index = (2 * pair + g) * GROUP + c
                    value = smoothed[k, pair, c * ROWS : (c + 1) * ROWS, g * NX : (g + 1) * NX]
                    value = value * scale[k, index : index + 1, :]
                    best = value if best is None else jnp.maximum(best, value)
        for i in range(copies):
            peaks[i, k] = best


def body(planes, widths):
    tiles, blocks = lax.axis_size("tile"), lax.axis_size("fblk")
    own = lax.all_to_all(planes, "tile", split_axis=1, concat_axis=0, tiled=True)
    channels = own.shape[0]
    cells = ROWS * tiles * NX
    a_high, a_low = map(jnp.asarray, split(vertical_matrix()))
    h_high, h_low = map(jnp.asarray, split(horizontal_matrices()))
    a_shape = jax.ShapeDtypeStruct(a_high.shape, BF)
    a_high, a_low = pl.pallas_call(
        mask_kernel, out_shape=[a_shape, a_shape], in_specs=[SMEM, VMEM, VMEM], out_specs=[VMEM, VMEM], compiler_params=PARAMS
    )(widths, a_high, a_low)
    up = [(i, i + 1) for i in range(tiles - 1)]
    down = [(i + 1, i) for i in range(tiles - 1)]
    before = lax.ppermute(own[:, ROWS - RAD :], "tile", up)
    after = lax.ppermute(own[:, :RAD], "tile", down)
    first = slice(0, MAXW - 1)
    edge = jnp.concatenate([before[first], own[first], after[first]], axis=1)
    edge = lax.ppermute(edge, "fblk", [(i + 1, i) for i in range(blocks - 1)])
    smoothed, sums = pl.pallas_call(
        smooth_kernel,
        out_shape=[
            jax.ShapeDtypeStruct((KERNELS, channels // (2 * GROUP), GROUP * ROWS, 2 * NX), F32),
            jax.ShapeDtypeStruct((2 * tiles, NX), F32),
        ],
        in_specs=[VMEM] * 8,
        out_specs=[VMEM] * 2,
        scratch_shapes=[pltpu.VMEM((channels + MAXW, SPAN, NX), BF)] * 2,
        compiler_params=PARAMS,
    )(own, before, after, edge, a_high, a_low, h_high, h_low)
    received = lax.all_to_all(sums, "tile", split_axis=0, concat_axis=0, tiled=True)
    peaks = pl.pallas_call(
        lambda *refs: peak_kernel(cells, blocks, *refs),
        out_shape=jax.ShapeDtypeStruct((blocks, KERNELS, ROWS, NX), F32),
        in_specs=[SMEM, VMEM, VMEM],
        out_specs=VMEM,
        scratch_shapes=[pltpu.VMEM((KERNELS, channels, NX), F32)],
        compiler_params=PARAMS,
    )(widths, received, smoothed)
    peaks = lax.all_to_all(peaks, "fblk", split_axis=0, concat_axis=0, tiled=True)
    return jnp.max(peaks, axis=0)


def solution(mesh):
    placed = (P(("fblk", "tile"), None, None), P())
    return jax.shard_map(body, mesh=mesh, in_specs=placed, out_specs=P(None, "tile", None), check_vma=False)
```

```python
import jax
import jax.numpy as jnp
import numpy as np
from jax import lax
from jax.experimental import pallas as pl
from jax.experimental.pallas import tpu as pltpu
from jax.sharding import PartitionSpec as P

KERNELS = 4
RAD = 8
MAXW = 8
SIGMAS = (1.0, 1.6, 2.3, 3.2)
EPSILON = 1e-06
ROWS = 16
SPAN = ROWS + 2 * RAD
GROUP = 8
NX = 128
BLOCK = GROUP * ROWS
BF = jnp.bfloat16
F32 = jnp.float32
VMEM = pl.BlockSpec(memory_space=pltpu.VMEM)
SMEM = pl.BlockSpec(memory_space=pltpu.SMEM)
PARAMS = pltpu.CompilerParams(vmem_limit_bytes=32 * 1024 * 1024)


def taps(sigma):
    offsets = np.arange(2 * RAD + 1) - RAD
    values = np.exp(-(offsets**2) / (2.0 * sigma * sigma))
    return values / values.sum()


def split(matrix):
    matrix = np.asarray(matrix, np.float32)
    high = matrix.astype(BF)
    return high, (matrix - high.astype(np.float32)).astype(BF)


def vertical_matrix():
    out = np.zeros((KERNELS, GROUP, ROWS, 2 * GROUP, SPAN))
    for k, sigma in enumerate(SIGMAS):
        weights = taps(sigma)
        for row in range(ROWS):
            for channel in range(GROUP):
                for offset in range(MAXW):
                    out[k, channel, row, channel + offset, row : row + 2 * RAD + 1] = weights
    return out.reshape(KERNELS * GROUP * ROWS, 2 * GROUP * SPAN)


def horizontal_matrices():
    out = np.zeros((KERNELS, 2, NX, 2, NX))
    for k, sigma in enumerate(SIGMAS):
        weights = taps(sigma)
        for x in range(NX):
            for j in range(-RAD, RAD + 1):
                if 0 <= x + j < NX:
                    out[k, :, x + j, :, x] = weights[j + RAD] * np.eye(2)
    return out.reshape(KERNELS, 2 * NX, 2 * NX)


def halves(values):
    high = values.astype(BF)
    return high, (values - high.astype(F32)).astype(BF)


def dot(a, b):
    return jnp.dot(a, b, preferred_element_type=F32)


def dot3(a_high, a_low, b_high, b_low):
    return dot(a_high, b_high) + (dot(a_low, b_high) + dot(a_high, b_low))


def lane_sums(rows):
    return lax.dot_general(
        jnp.ones((8, NX), F32), rows, (((1,), (1,)), ((), ())), precision=lax.Precision.HIGHEST, preferred_element_type=F32
    )


def row_squares(values):
    return jnp.sum((values * values).reshape(GROUP, ROWS, values.shape[1]), axis=1)


def mask_kernel(widths, high_in, low_in, high, low):
    shape = (BLOCK, 2 * GROUP * SPAN)
    offset = lax.broadcasted_iota(jnp.int32, shape, 1) // SPAN - lax.broadcasted_iota(jnp.int32, shape, 0) // ROWS
    for k in range(KERNELS):
        keep = jnp.where(offset < widths[k], 1.0, 0.0)
        rows = pl.ds(k * BLOCK, BLOCK)
        high[rows, :] = (high_in[rows, :].astype(F32) * keep).astype(BF)
        low[rows, :] = (low_in[rows, :].astype(F32) * keep).astype(BF)


def framed(parity, own, flip, off):
    even = parity == 0
    return jnp.concatenate([jnp.where(even, off, flip), own, jnp.where(even, flip, off)], axis=1)


def main_kernel(parity, own, flip, off, a_high, a_low, h_high, h_low, smoothed, rest, sums, x_high, x_low, y_high, y_low):
    channels = own.shape[0]
    groups = channels // GROUP
    pairs = groups // 2
    x_high[0:channels], x_low[0:channels] = halves(framed(parity[0], own[...], flip[...], off[...]))
    x_high[channels:] = jnp.zeros((GROUP, SPAN, NX), BF)
    x_low[channels:] = jnp.zeros((GROUP, SPAN, NX), BF)
    for pair in range(pairs):

        def side_by_side(ref):
            first = 2 * pair * GROUP
            parts = [ref[first + s : first + s + 2 * GROUP].reshape(2 * GROUP * SPAN, NX) for s in (0, GROUP)]
            return jnp.concatenate(parts, axis=1)

        y = dot3(a_high[...], a_low[...], side_by_side(x_high), side_by_side(x_low))
        if pair == pairs - 1:
            rest[...] = y[:, NX:]
        yh, yl = halves(y)
        for k in range(KERNELS):
            y_high[k, pair * BLOCK : (pair + 1) * BLOCK] = yh[k * BLOCK : (k + 1) * BLOCK]
            y_low[k, pair * BLOCK : (pair + 1) * BLOCK] = yl[k * BLOCK : (k + 1) * BLOCK]
    squares = []
    for k in range(KERNELS):
        z = dot3(y_high[k], y_low[k], h_high[k], h_low[k])
        for pair in range(pairs):
            part = z[pair * BLOCK : (pair + 1) * BLOCK]
            smoothed[k, pair] = part
            squared = row_squares(part)
            squares += [squared[:, :NX], squared[:, NX:]][: groups - 1 - 2 * pair]
    squares.append(jnp.zeros((KERNELS * GROUP, NX), F32))
    sums[...] = lane_sums(jnp.concatenate(squares, axis=0))


def tail_kernel(parity, own, flip, off, a_high, a_low, h_high, h_low, rest, main_sums, smoothed, sums):
    x = framed(parity[0], own[...], flip[...], off[...])
    x = jnp.concatenate([x, jnp.zeros((1, SPAN, NX), F32)], axis=0)
    xh, xl = halves(x.reshape(GROUP * SPAN, NX))
    late = slice(GROUP * SPAN, 2 * GROUP * SPAN)
    yh, yl = halves(rest[...] + dot3(a_high[:, late], a_low[:, late], xh, xl))
    squares = [jnp.zeros((NX - KERNELS * GROUP, NX), F32)]
    for k in range(KERNELS):
        rows = slice(k * BLOCK, (k + 1) * BLOCK)
        z = dot3(yh[rows], yl[rows], h_high[k, :NX, :NX], h_low[k, :NX, :NX])
        smoothed[k] = z
        squares.append(row_squares(z))
    total = lane_sums(jnp.concatenate(squares, axis=0))
    low = jnp.broadcast_to(main_sums[0:1, :NX], sums.shape)
    high = jnp.broadcast_to(main_sums[0:1, NX:] + total[0:1], sums.shape)
    sums[...] = jnp.where(lax.broadcasted_iota(jnp.int32, sums.shape, 0) % 2 == 0, low, high)


def peak_kernel(cells, copies, widths, received, smoothed, last, peaks, scale):
    groups = 2 * smoothed.shape[1]
    per_kernel = (groups - 1) * GROUP
    row_odd = lax.broadcasted_iota(jnp.int32, (received.shape[0], NX), 0) % 2
    for h in (0, 1):
        scale[h * NX : (h + 1) * NX, :] = lax.dot_general(
            received[...],
            jnp.where(row_odd == h, 1.0, 0.0),
            (((0,), (0,)), ((), ())),
            precision=lax.Precision.HIGHEST,
            preferred_element_type=F32,
        )
    for k in range(KERNELS):
        floor = widths[k].astype(F32) * EPSILON
        spans = ((k * per_kernel, per_kernel), (KERNELS * per_kernel + k * GROUP, GROUP))
        inverse = [1.0 / jnp.sqrt(scale[at : at + size, :] * (1.0 / cells) + floor) for at, size in spans]
        best = None
        for group in range(groups):
            for c in range(GROUP):
                rows = slice(c * ROWS, (c + 1) * ROWS)
                if group < groups - 1:
                    lanes = slice((group % 2) * NX, (group % 2 + 1) * NX)
                    value = smoothed[k, group // 2, rows, lanes] * inverse[0][group * GROUP + c : group * GROUP + c + 1]
                else:
                    value = last[k, rows] * inverse[1][c : c + 1]
                best = value if best is None else jnp.maximum(best, value)
        for i in range(copies):
            peaks[i, k] = best


def call(kernel, out_shape, in_specs, scratch=(), flops=0, moved=0):
    return pl.pallas_call(
        kernel,
        out_shape=out_shape,
        in_specs=in_specs,
        out_specs=jax.tree.map(lambda _: VMEM, out_shape),
        scratch_shapes=list(scratch),
        compiler_params=PARAMS,
        cost_estimate=pl.CostEstimate(flops=flops, bytes_accessed=moved, transcendentals=0),
    )


def body(planes, widths):
    tiles, blocks = lax.axis_size("tile"), lax.axis_size("fblk")
    shape = jax.ShapeDtypeStruct
    parity = jnp.reshape(lax.axis_index("tile") % 2, (1,)).astype(jnp.int32)
    own = lax.all_to_all(planes, "tile", split_axis=1, concat_axis=0, tiled=True)
    channels = own.shape[0]
    pairs = channels // (2 * GROUP)
    cells = ROWS * tiles * NX
    a_high, a_low = map(jnp.asarray, split(vertical_matrix()))
    h_high, h_low = map(jnp.asarray, split(horizontal_matrices()))
    a_shape = shape(a_high.shape, BF)
    a_high, a_low = call(mask_kernel, [a_shape, a_shape], [SMEM, VMEM, VMEM], moved=2**21)(widths, a_high, a_low)

    odd = parity[0] == 1
    top, bottom = own[:, :RAD], own[:, ROWS - RAD :]
    inner = [(i + 1, i + 2) for i in range(0, tiles - 2, 2)]
    off = lax.ppermute(jnp.where(odd, bottom, top), "tile", inner + [(b, a) for a, b in inner])
    flip = lax.ppermute(jnp.where(odd, top, bottom), "tile", [(i, i ^ 1) for i in range(tiles)])
    first = slice(0, MAXW - 1)
    edge = jnp.concatenate([flip[first], own[first], off[first]], axis=1)
    edge = lax.ppermute(edge, "fblk", [(i + 1, i) for i in range(blocks - 1)])

    matrices = (a_high, a_low, h_high, h_low)
    smoothed, rest, sums = call(
        main_kernel,
        [
            shape((KERNELS, pairs, BLOCK, 2 * NX), F32),
            shape((KERNELS * BLOCK, NX), F32),
            shape((8, KERNELS * channels), F32),
        ],
        [SMEM] + [VMEM] * 7,
        [pltpu.VMEM((channels + GROUP, SPAN, NX), BF)] * 2 + [pltpu.VMEM((KERNELS, pairs * BLOCK, 2 * NX), BF)] * 2,
        flops=2**32,
        moved=2**23,
    )(parity, own, flip, off, *matrices)
    last, sums = call(
        tail_kernel,
        [shape((KERNELS, BLOCK, NX), F32), shape((2 * tiles, NX), F32)],
        [SMEM] + [VMEM] * 9,
        flops=2**29,
        moved=2**20,
    )(parity, edge[:, RAD : RAD + ROWS], edge[:, :RAD], edge[:, RAD + ROWS :], *matrices, rest, sums)
    received = lax.all_to_all(sums, "tile", split_axis=0, concat_axis=0, tiled=True)
    peaks = call(
        lambda *refs: peak_kernel(cells, blocks, *refs),
        shape((blocks, KERNELS, ROWS, NX), F32),
        [SMEM] + [VMEM] * 3,
        [pltpu.VMEM((KERNELS * channels, NX), F32)],
        moved=2**22,
    )(widths, received, smoothed, last)
    peaks = lax.all_to_all(peaks, "fblk", split_axis=0, concat_axis=0, tiled=True)
    return jnp.max(peaks, axis=0)


def solution(mesh):
    placed = (P(("fblk", "tile"), None, None), P())
    return jax.shard_map(body, mesh=mesh, in_specs=placed, out_specs=P(None, "tile", None), check_vma=False)
```

```python
import jax
import jax.numpy as jnp
import numpy as np
from jax import lax
from jax.experimental import pallas as pl
from jax.experimental.pallas import tpu as pltpu
from jax.sharding import PartitionSpec as P

KERNELS = 4
RAD = 8
MAXW = 8
SIGMAS = (1.0, 1.6, 2.3, 3.2)
EPSILON = 1e-06
ROWS = 16
SPAN = ROWS + 2 * RAD
GROUP = 8
NX = 128
BLOCK = GROUP * ROWS
BF = jnp.bfloat16
F32 = jnp.float32
VMEM = pl.BlockSpec(memory_space=pltpu.VMEM)
SMEM = pl.BlockSpec(memory_space=pltpu.SMEM)
PARAMS = pltpu.CompilerParams(vmem_limit_bytes=32 * 1024 * 1024)


def taps(sigma):
    offsets = np.arange(2 * RAD + 1) - RAD
    values = np.exp(-(offsets**2) / (2.0 * sigma * sigma))
    return values / values.sum()


def split(matrix):
    matrix = np.asarray(matrix, np.float32)
    high = matrix.astype(BF)
    return high, (matrix - high.astype(np.float32)).astype(BF)


def vertical_matrix():
    out = np.zeros((KERNELS, GROUP, ROWS, 2 * GROUP, SPAN))
    for k, sigma in enumerate(SIGMAS):
        weights = taps(sigma)
        for row in range(ROWS):
            for channel in range(GROUP):
                for offset in range(MAXW):
                    out[k, channel, row, channel + offset, row : row + 2 * RAD + 1] = weights
    return out.reshape(KERNELS * GROUP * ROWS, 2 * GROUP * SPAN)


def horizontal_matrices():
    out = np.zeros((KERNELS, 2, NX, 2, NX))
    for k, sigma in enumerate(SIGMAS):
        weights = taps(sigma)
        for x in range(NX):
            for j in range(-RAD, RAD + 1):
                if 0 <= x + j < NX:
                    out[k, :, x + j, :, x] = weights[j + RAD] * np.eye(2)
    return out.reshape(KERNELS, 2 * NX, 2 * NX)


def halves(values):
    high = values.astype(BF)
    return high, (values - high.astype(F32)).astype(BF)


def dot(a, b):
    return jnp.dot(a, b, preferred_element_type=F32)


def dot3(a_high, a_low, b_high, b_low):
    return dot(a_high, b_high) + (dot(a_low, b_high) + dot(a_high, b_low))


def lane_sums(rows):
    return lax.dot_general(
        jnp.ones((8, NX), F32), rows, (((1,), (1,)), ((), ())), precision=lax.Precision.HIGHEST, preferred_element_type=F32
    )


def row_squares(values):
    return jnp.sum((values * values).reshape(GROUP, ROWS, values.shape[1]), axis=1)


def mask_kernel(widths, high_in, low_in, high, low):
    shape = (BLOCK, 2 * GROUP * SPAN)
    offset = lax.broadcasted_iota(jnp.int32, shape, 1) // SPAN - lax.broadcasted_iota(jnp.int32, shape, 0) // ROWS
    for k in range(KERNELS):
        keep = jnp.where(offset < widths[k], 1.0, 0.0)
        rows = pl.ds(k * BLOCK, BLOCK)
        high[rows, :] = (high_in[rows, :].astype(F32) * keep).astype(BF)
        low[rows, :] = (low_in[rows, :].astype(F32) * keep).astype(BF)


def framed(parity, own, off, flip):
    even = parity == 0
    return jnp.concatenate([jnp.where(even, off, flip), own, jnp.where(even, flip, off)], axis=1)


def main_kernel(parity, own, off, flip, a_high, a_low, h_high, h_low, smoothed, rest, sums, x_high, x_low, y_high, y_low):
    channels = own.shape[0]
    groups = channels // GROUP
    pairs = groups // 2
    x_high[0:channels], x_low[0:channels] = halves(framed(parity[0], own[...], off[...], flip[...]))
    x_high[channels:] = jnp.zeros((GROUP, SPAN, NX), BF)
    x_low[channels:] = jnp.zeros((GROUP, SPAN, NX), BF)
    for pair in range(pairs):

        def side_by_side(ref):
            first = 2 * pair * GROUP
            parts = [ref[first + s : first + s + 2 * GROUP].reshape(2 * GROUP * SPAN, NX) for s in (0, GROUP)]
            return jnp.concatenate(parts, axis=1)

        y = dot3(a_high[...], a_low[...], side_by_side(x_high), side_by_side(x_low))
        if pair == pairs - 1:
            rest[...] = y[:, NX:]
        yh, yl = halves(y)
        for k in range(KERNELS):
            y_high[k, pair * BLOCK : (pair + 1) * BLOCK] = yh[k * BLOCK : (k + 1) * BLOCK]
            y_low[k, pair * BLOCK : (pair + 1) * BLOCK] = yl[k * BLOCK : (k + 1) * BLOCK]
    squares = []
    for k in range(KERNELS):
        z = dot3(y_high[k], y_low[k], h_high[k], h_low[k])
        for pair in range(pairs):
            part = z[pair * BLOCK : (pair + 1) * BLOCK]
            smoothed[k, pair] = part
            squared = row_squares(part)
            squares += [squared[:, :NX], squared[:, NX:]][: groups - 1 - 2 * pair]
    squares.append(jnp.zeros((KERNELS * GROUP, NX), F32))
    sums[...] = lane_sums(jnp.concatenate(squares, axis=0))


def tail_kernel(parity, own, off, flip, a_high, a_low, h_high, h_low, rest, main_sums, smoothed, sums):
    x = framed(parity[0], own[...], off[...], flip[...])
    x = jnp.concatenate([x, jnp.zeros((1, SPAN, NX), F32)], axis=0)
    xh, xl = halves(x.reshape(GROUP * SPAN, NX))
    late = slice(GROUP * SPAN, 2 * GROUP * SPAN)
    yh, yl = halves(rest[...] + dot3(a_high[:, late], a_low[:, late], xh, xl))
    squares = [jnp.zeros((NX - KERNELS * GROUP, NX), F32)]
    for k in range(KERNELS):
        rows = slice(k * BLOCK, (k + 1) * BLOCK)
        z = dot3(yh[rows], yl[rows], h_high[k, :NX, :NX], h_low[k, :NX, :NX])
        smoothed[k] = z
        squares.append(row_squares(z))
    total = lane_sums(jnp.concatenate(squares, axis=0))
    low = jnp.broadcast_to(main_sums[0:1, :NX], sums.shape)
    high = jnp.broadcast_to(main_sums[0:1, NX:] + total[0:1], sums.shape)
    sums[...] = jnp.where(lax.broadcasted_iota(jnp.int32, sums.shape, 0) % 2 == 0, low, high)


def peak_kernel(cells, copies, widths, received, smoothed, last, peaks, scale):
    groups = 2 * smoothed.shape[1]
    per_kernel = (groups - 1) * GROUP
    row_odd = lax.broadcasted_iota(jnp.int32, (received.shape[0], NX), 0) % 2
    for h in (0, 1):
        scale[h * NX : (h + 1) * NX, :] = lax.dot_general(
            received[...],
            jnp.where(row_odd == h, 1.0, 0.0),
            (((0,), (0,)), ((), ())),
            precision=lax.Precision.HIGHEST,
            preferred_element_type=F32,
        )
    for k in range(KERNELS):
        floor = widths[k].astype(F32) * EPSILON
        spans = ((k * per_kernel, per_kernel), (KERNELS * per_kernel + k * GROUP, GROUP))
        inverse = [1.0 / jnp.sqrt(scale[at : at + size, :] * (1.0 / cells) + floor) for at, size in spans]
        best = None
        for group in range(groups):
            for c in range(GROUP):
                rows = slice(c * ROWS, (c + 1) * ROWS)
                if group < groups - 1:
                    lanes = slice((group % 2) * NX, (group % 2 + 1) * NX)
                    value = smoothed[k, group // 2, rows, lanes] * inverse[0][group * GROUP + c : group * GROUP + c + 1]
                else:
                    value = last[k, rows] * inverse[1][c : c + 1]
                best = value if best is None else jnp.maximum(best, value)
        for i in range(copies):
            peaks[i, k] = best


def call(kernel, out_shape, in_specs, scratch=(), flops=0, moved=0):
    return pl.pallas_call(
        kernel,
        out_shape=out_shape,
        in_specs=in_specs,
        out_specs=jax.tree.map(lambda _: VMEM, out_shape),
        scratch_shapes=list(scratch),
        compiler_params=PARAMS,
        cost_estimate=pl.CostEstimate(flops=flops, bytes_accessed=moved, transcendentals=0),
    )


def body(planes, widths):
    tiles, blocks = lax.axis_size("tile"), lax.axis_size("fblk")
    shape = jax.ShapeDtypeStruct
    parity = jnp.reshape(lax.axis_index("tile") % 2, (1,)).astype(jnp.int32)
    own = lax.all_to_all(planes, "tile", split_axis=1, concat_axis=0, tiled=True)
    channels = own.shape[0]
    pairs = channels // (2 * GROUP)
    cells = ROWS * tiles * NX
    a_high, a_low = map(jnp.asarray, split(vertical_matrix()))
    h_high, h_low = map(jnp.asarray, split(horizontal_matrices()))
    a_shape = shape(a_high.shape, BF)
    a_high, a_low = call(mask_kernel, [a_shape, a_shape], [SMEM, VMEM, VMEM], moved=2**21)(widths, a_high, a_low)

    odd = parity[0] == 1
    top, bottom = own[:, :RAD], own[:, ROWS - RAD :]
    inner = [(i + 1, i + 2) for i in range(0, tiles - 2, 2)]
    off = lax.ppermute(jnp.where(odd, bottom, top), "tile", inner + [(b, a) for a, b in inner])
    flip = lax.ppermute(jnp.where(odd, top, bottom), "tile", [(i, i ^ 1) for i in range(tiles)])
    first = slice(0, MAXW - 1)
    edge = jnp.concatenate([off[first], own[first], flip[first]], axis=1)
    edge = lax.ppermute(edge, "fblk", [(i + 1, i) for i in range(blocks - 1)])

    matrices = (a_high, a_low, h_high, h_low)
    smoothed, rest, sums = call(
        main_kernel,
        [
            shape((KERNELS, pairs, BLOCK, 2 * NX), F32),
            shape((KERNELS * BLOCK, NX), F32),
            shape((8, KERNELS * channels), F32),
        ],
        [SMEM] + [VMEM] * 7,
        [pltpu.VMEM((channels + GROUP, SPAN, NX), BF)] * 2 + [pltpu.VMEM((KERNELS, pairs * BLOCK, 2 * NX), BF)] * 2,
        flops=2**32,
        moved=2**23,
    )(parity, own, off, flip, *matrices)
    last, sums = call(
        tail_kernel,
        [shape((KERNELS, BLOCK, NX), F32), shape((2 * tiles, NX), F32)],
        [SMEM] + [VMEM] * 9,
        flops=2**29,
        moved=2**20,
    )(parity, edge[:, RAD : RAD + ROWS], edge[:, :RAD], edge[:, RAD + ROWS :], *matrices, rest, sums)
    received = lax.all_to_all(sums, "tile", split_axis=0, concat_axis=0, tiled=True)
    peaks = call(
        lambda *refs: peak_kernel(cells, blocks, *refs),
        shape((blocks, KERNELS, ROWS, NX), F32),
        [SMEM] + [VMEM] * 3,
        [pltpu.VMEM((KERNELS * channels, NX), F32)],
        moved=2**22,
    )(widths, received, smoothed, last)
    peaks = lax.all_to_all(peaks, "fblk", split_axis=0, concat_axis=0, tiled=True)
    return jnp.max(peaks, axis=0)


def solution(mesh):
    placed = (P(("fblk", "tile"), None, None), P())
    return jax.shard_map(body, mesh=mesh, in_specs=placed, out_specs=P(None, "tile", None), check_vma=False)
```

```python
import jax
import jax.numpy as jnp
import numpy as np
from jax import lax
from jax.experimental import pallas as pl
from jax.experimental.pallas import tpu as pltpu
from jax.sharding import PartitionSpec as P

KERNELS = 4
RAD = 8
MAXW = 8
SIGMAS = (1.0, 1.6, 2.3, 3.2)
EPSILON = 1e-06
ROWS = 16
SPAN = ROWS + 2 * RAD
GROUP = 8
NX = 128
BLOCK = GROUP * ROWS
BF = jnp.bfloat16
F32 = jnp.float32
VMEM = pl.BlockSpec(memory_space=pltpu.VMEM)
SMEM = pl.BlockSpec(memory_space=pltpu.SMEM)
PARAMS = pltpu.CompilerParams(vmem_limit_bytes=32 * 1024 * 1024)


def taps(sigma):
    offsets = np.arange(2 * RAD + 1) - RAD
    values = np.exp(-(offsets**2) / (2.0 * sigma * sigma))
    return values / values.sum()


def split(matrix):
    matrix = np.asarray(matrix, np.float32)
    high = matrix.astype(BF)
    return high, (matrix - high.astype(np.float32)).astype(BF)


def vertical_matrix():
    out = np.zeros((KERNELS, GROUP, ROWS, 2 * GROUP, SPAN))
    for k, sigma in enumerate(SIGMAS):
        weights = taps(sigma)
        for row in range(ROWS):
            for channel in range(GROUP):
                for offset in range(MAXW):
                    out[k, channel, row, channel + offset, row : row + 2 * RAD + 1] = weights
    return out.reshape(KERNELS * GROUP * ROWS, 2 * GROUP * SPAN)


def horizontal_matrices():
    out = np.zeros((KERNELS, 2, NX, 2, NX))
    for k, sigma in enumerate(SIGMAS):
        weights = taps(sigma)
        for x in range(NX):
            for j in range(-RAD, RAD + 1):
                if 0 <= x + j < NX:
                    out[k, :, x + j, :, x] = weights[j + RAD] * np.eye(2)
    return out.reshape(KERNELS, 2 * NX, 2 * NX)


def halves(values):
    high = values.astype(BF)
    return high, (values - high.astype(F32)).astype(BF)


def dot(a, b):
    return jnp.dot(a, b, preferred_element_type=F32)


def dot3(a_high, a_low, b_high, b_low):
    return dot(a_high, b_high) + (dot(a_low, b_high) + dot(a_high, b_low))


def lane_sums(rows):
    return lax.dot_general(
        jnp.ones((8, NX), F32), rows, (((1,), (1,)), ((), ())), precision=lax.Precision.HIGHEST, preferred_element_type=F32
    )


def row_squares(values):
    return jnp.sum((values * values).reshape(GROUP, ROWS, values.shape[1]), axis=1)


def mask_kernel(widths, high_in, low_in, high, low):
    shape = (BLOCK, 2 * GROUP * SPAN)
    offset = lax.broadcasted_iota(jnp.int32, shape, 1) // SPAN - lax.broadcasted_iota(jnp.int32, shape, 0) // ROWS
    for k in range(KERNELS):
        keep = jnp.where(offset < widths[k], 1.0, 0.0)
        rows = pl.ds(k * BLOCK, BLOCK)
        high[rows, :] = (high_in[rows, :].astype(F32) * keep).astype(BF)
        low[rows, :] = (low_in[rows, :].astype(F32) * keep).astype(BF)


def framed(parity, own, off, flip):
    even = parity == 0
    return jnp.concatenate([jnp.where(even, off, flip), own, jnp.where(even, flip, off)], axis=1)


def main_kernel(parity, own, off, flip, a_high, a_low, h_high, h_low, smoothed, rest, sums, x_high, x_low, y_high, y_low):
    channels = own.shape[0]
    groups = channels // GROUP
    pairs = groups // 2
    x_high[0:channels], x_low[0:channels] = halves(framed(parity[0], own[...], off[...], flip[...]))
    x_high[channels:] = jnp.zeros((GROUP, SPAN, NX), BF)
    x_low[channels:] = jnp.zeros((GROUP, SPAN, NX), BF)
    for pair in range(pairs):

        def side_by_side(ref):
            first = 2 * pair * GROUP
            parts = [ref[first + s : first + s + 2 * GROUP].reshape(2 * GROUP * SPAN, NX) for s in (0, GROUP)]
            return jnp.concatenate(parts, axis=1)

        y = dot3(a_high[...], a_low[...], side_by_side(x_high), side_by_side(x_low))
        if pair == pairs - 1:
            rest[...] = y[:, NX:]
        yh, yl = halves(y)
        for k in range(KERNELS):
            y_high[k, pair * BLOCK : (pair + 1) * BLOCK] = yh[k * BLOCK : (k + 1) * BLOCK]
            y_low[k, pair * BLOCK : (pair + 1) * BLOCK] = yl[k * BLOCK : (k + 1) * BLOCK]
    squares = []
    for k in range(KERNELS):
        z = dot3(y_high[k], y_low[k], h_high[k], h_low[k])
        for pair in range(pairs):
            part = z[pair * BLOCK : (pair + 1) * BLOCK]
            smoothed[k, pair] = part
            squared = row_squares(part)
            squares += [squared[:, :NX], squared[:, NX:]][: groups - 1 - 2 * pair]
    squares.append(jnp.zeros((KERNELS * GROUP, NX), F32))
    sums[...] = lane_sums(jnp.concatenate(squares, axis=0))


def tail_kernel(parity, own, off, flip, a_high, a_low, h_high, h_low, rest, main_sums, smoothed, sums):
    x = framed(parity[0], own[...], off[...], flip[...])
    x = jnp.concatenate([x, jnp.zeros((1, SPAN, NX), F32)], axis=0)
    xh, xl = halves(x.reshape(GROUP * SPAN, NX))
    late = slice(GROUP * SPAN, 2 * GROUP * SPAN)
    yh, yl = halves(rest[...] + dot3(a_high[:, late], a_low[:, late], xh, xl))
    squares = [jnp.zeros((NX - KERNELS * GROUP, NX), F32)]
    for k in range(KERNELS):
        rows = slice(k * BLOCK, (k + 1) * BLOCK)
        z = dot3(yh[rows], yl[rows], h_high[k, :NX, :NX], h_low[k, :NX, :NX])
        smoothed[k] = z
        squares.append(row_squares(z))
    total = lane_sums(jnp.concatenate(squares, axis=0))
    low = jnp.broadcast_to(main_sums[0:1, :NX], sums.shape)
    high = jnp.broadcast_to(main_sums[0:1, NX:] + total[0:1], sums.shape)
    sums[...] = jnp.where(lax.broadcasted_iota(jnp.int32, sums.shape, 0) % 2 == 0, low, high)


def peak_kernel(cells, copies, widths, received, smoothed, last, peaks, scale):
    groups = 2 * smoothed.shape[1]
    per_kernel = (groups - 1) * GROUP
    row_odd = lax.broadcasted_iota(jnp.int32, (received.shape[0], NX), 0) % 2
    for h in (0, 1):
        scale[h * NX : (h + 1) * NX, :] = lax.dot_general(
            received[...],
            jnp.where(row_odd == h, 1.0, 0.0),
            (((0,), (0,)), ((), ())),
            precision=lax.Precision.HIGHEST,
            preferred_element_type=F32,
        )
    for k in range(KERNELS):
        floor = widths[k].astype(F32) * EPSILON
        spans = ((k * per_kernel, per_kernel), (KERNELS * per_kernel + k * GROUP, GROUP))
        inverse = [1.0 / jnp.sqrt(scale[at : at + size, :] * (1.0 / cells) + floor) for at, size in spans]
        best = None
        for group in range(groups):
            for c in range(GROUP):
                rows = slice(c * ROWS, (c + 1) * ROWS)
                if group < groups - 1:
                    lanes = slice((group % 2) * NX, (group % 2 + 1) * NX)
                    value = smoothed[k, group // 2, rows, lanes] * inverse[0][group * GROUP + c : group * GROUP + c + 1]
                else:
                    value = last[k, rows] * inverse[1][c : c + 1]
                best = value if best is None else jnp.maximum(best, value)
        for i in range(copies):
            peaks[i, k] = best


def call(kernel, out_shape, in_specs, scratch=(), flops=0, moved=0):
    return pl.pallas_call(
        kernel,
        out_shape=out_shape,
        in_specs=in_specs,
        out_specs=jax.tree.map(lambda _: VMEM, out_shape),
        scratch_shapes=list(scratch),
        compiler_params=PARAMS,
        cost_estimate=pl.CostEstimate(flops=flops, bytes_accessed=moved, transcendentals=0),
    )


def body(planes, widths):
    tiles, blocks = lax.axis_size("tile"), lax.axis_size("fblk")
    shape = jax.ShapeDtypeStruct
    parity = jnp.reshape(lax.axis_index("tile") % 2, (1,)).astype(jnp.int32)
    own = lax.all_to_all(planes, "tile", split_axis=1, concat_axis=0, tiled=True)
    channels = own.shape[0]
    pairs = channels // (2 * GROUP)
    cells = ROWS * tiles * NX
    a_high, a_low = map(jnp.asarray, split(vertical_matrix()))
    h_high, h_low = map(jnp.asarray, split(horizontal_matrices()))
    a_shape = shape(a_high.shape, BF)
    a_high, a_low = call(mask_kernel, [a_shape, a_shape], [SMEM, VMEM, VMEM], moved=2**21)(widths, a_high, a_low)
    own, a_high, a_low = lax.optimization_barrier((own, a_high, a_low))

    odd = parity[0] == 1
    top, bottom = own[:, :RAD], own[:, ROWS - RAD :]
    inner = [(i + 1, i + 2) for i in range(0, tiles - 2, 2)]
    off = lax.ppermute(jnp.where(odd, bottom, top), "tile", inner + [(b, a) for a, b in inner])
    flip = lax.ppermute(jnp.where(odd, top, bottom), "tile", [(i, i ^ 1) for i in range(tiles)])
    first = slice(0, MAXW - 1)
    edge = jnp.concatenate([off[first], own[first], flip[first]], axis=1)
    edge = lax.ppermute(edge, "fblk", [(i + 1, i) for i in range(blocks - 1)])

    matrices = (a_high, a_low, h_high, h_low)
    smoothed, rest, sums = call(
        main_kernel,
        [
            shape((KERNELS, pairs, BLOCK, 2 * NX), F32),
            shape((KERNELS * BLOCK, NX), F32),
            shape((8, KERNELS * channels), F32),
        ],
        [SMEM] + [VMEM] * 7,
        [pltpu.VMEM((channels + GROUP, SPAN, NX), BF)] * 2 + [pltpu.VMEM((KERNELS, pairs * BLOCK, 2 * NX), BF)] * 2,
        flops=2**32,
        moved=2**23,
    )(parity, own, off, flip, *matrices)
    last, sums = call(
        tail_kernel,
        [shape((KERNELS, BLOCK, NX), F32), shape((2 * tiles, NX), F32)],
        [SMEM] + [VMEM] * 9,
        flops=2**29,
        moved=2**20,
    )(parity, edge[:, RAD : RAD + ROWS], edge[:, :RAD], edge[:, RAD + ROWS :], *matrices, rest, sums)
    received = lax.all_to_all(
        sums, "tile", split_axis=0, concat_axis=0, tiled=True, axis_index_groups=[list(range(tiles))[::-1]]
    )
    peaks = call(
        lambda *refs: peak_kernel(cells, blocks, *refs),
        shape((blocks, KERNELS, ROWS, NX), F32),
        [SMEM] + [VMEM] * 3,
        [pltpu.VMEM((KERNELS * channels, NX), F32)],
        moved=2**22,
    )(widths, received, smoothed, last)
    peaks = lax.all_to_all(
        peaks, "fblk", split_axis=0, concat_axis=0, tiled=True, axis_index_groups=[list(range(blocks))[::-1]]
    )
    return jnp.max(peaks, axis=0)


def solution(mesh):
    placed = (P(("fblk", "tile"), None, None), P())
    return jax.shard_map(body, mesh=mesh, in_specs=placed, out_specs=P(None, "tile", None), check_vma=False)
```

```python
import jax
import jax.numpy as jnp
import numpy as np
from jax import lax
from jax.experimental import pallas as pl
from jax.experimental.pallas import tpu as pltpu
from jax.sharding import PartitionSpec as P

KERNELS = 4
RAD = 8
MAXW = 8
SIGMAS = (1.0, 1.6, 2.3, 3.2)
EPSILON = 1e-06
ROWS = 16
GROUP = 8
NX = 128
BLOCK = GROUP * ROWS
DEPTH = 2 * GROUP * ROWS
BF = jnp.bfloat16
F32 = jnp.float32
VMEM = pl.BlockSpec(memory_space=pltpu.VMEM)
SMEM = pl.BlockSpec(memory_space=pltpu.SMEM)
PARAMS = pltpu.CompilerParams(vmem_limit_bytes=32 * 1024 * 1024)


def taps(sigma):
    offsets = np.arange(2 * RAD + 1) - RAD
    values = np.exp(-(offsets**2) / (2.0 * sigma * sigma))
    return values / values.sum()


def split(matrix):
    matrix = np.asarray(matrix, np.float32)
    high = matrix.astype(BF)
    return high, (matrix - high.astype(np.float32)).astype(BF)


def vertical_matrix():
    out = np.zeros((KERNELS, GROUP, ROWS, 2 * GROUP, ROWS + 2 * RAD))
    for k, sigma in enumerate(SIGMAS):
        weights = taps(sigma)
        for row in range(ROWS):
            for channel in range(GROUP):
                for offset in range(MAXW):
                    out[k, channel, row, channel + offset, row : row + 2 * RAD + 1] = weights
    own = out[..., RAD : RAD + ROWS]
    border = np.concatenate([out[..., :RAD], out[..., RAD + ROWS :]], axis=-1)
    return np.concatenate([x.reshape(KERNELS * BLOCK, DEPTH) for x in (own, border)], axis=1)


def horizontal_matrices():
    out = np.zeros((KERNELS, 2, NX, 2, NX))
    for k, sigma in enumerate(SIGMAS):
        weights = taps(sigma)
        for x in range(NX):
            for j in range(-RAD, RAD + 1):
                if 0 <= x + j < NX:
                    out[k, :, x + j, :, x] = weights[j + RAD] * np.eye(2)
    return out.reshape(KERNELS, 2 * NX, 2 * NX)


def halves(values):
    high = values.astype(BF)
    return high, (values - high.astype(F32)).astype(BF)


def dot(a, b):
    return jnp.dot(a, b, preferred_element_type=F32)


def dot3(a_high, a_low, b_high, b_low):
    return dot(a_high, b_high) + (dot(a_low, b_high) + dot(a_high, b_low))


def lane_sums(rows):
    ones = jnp.ones((8, NX), BF)
    parts = [
        lax.dot_general(ones, half, (((1,), (1,)), ((), ())), preferred_element_type=F32) for half in halves(rows)
    ]
    return parts[0] + parts[1]


def row_squares(values):
    return jnp.sum((values * values).reshape(GROUP, ROWS, values.shape[1]), axis=1)


def mask_kernel(widths, high_in, low_in, high, low):
    shape = (BLOCK, 2 * DEPTH)
    column = lax.broadcasted_iota(jnp.int32, shape, 1) % DEPTH
    offset = column // ROWS - lax.broadcasted_iota(jnp.int32, shape, 0) // ROWS
    for k in range(KERNELS):
        keep = jnp.where(offset < widths[k], 1.0, 0.0)
        rows = pl.ds(k * BLOCK, BLOCK)
        high[rows, :] = (high_in[rows, :].astype(F32) * keep).astype(BF)
        low[rows, :] = (low_in[rows, :].astype(F32) * keep).astype(BF)


def border_rows(parity, off, flip):
    even = parity == 0
    return jnp.concatenate([jnp.where(even, off, flip), jnp.where(even, flip, off)], axis=1)


def fill(values, high, low):
    channels = values.shape[0]
    high[0:channels], low[0:channels] = halves(values)
    high[channels:] = jnp.zeros((GROUP, ROWS, NX), BF)
    low[channels:] = jnp.zeros((GROUP, ROWS, NX), BF)


def side_by_side(ref, pair):
    first = 2 * pair * GROUP
    parts = [ref[first + s : first + s + 2 * GROUP].reshape(DEPTH, NX) for s in (0, GROUP)]
    return jnp.concatenate(parts, axis=1)


def own_kernel(own, a_high, a_low, partial, x_high, x_low):
    fill(own[...], x_high, x_low)
    for pair in range(partial.shape[0]):
        xs = side_by_side(x_high, pair), side_by_side(x_low, pair)
        partial[pair] = dot3(a_high[:, :DEPTH], a_low[:, :DEPTH], *xs)


def main_kernel(parity, off, flip, partial, a_high, a_low, h_high, h_low, smoothed, rest, sums, x_high, x_low, y_high, y_low):
    pairs = partial.shape[0]
    groups = 2 * pairs
    fill(border_rows(parity[0], off[...], flip[...]), x_high, x_low)
    for pair in range(pairs):
        xs = side_by_side(x_high, pair), side_by_side(x_low, pair)
        y = partial[pair] + dot3(a_high[:, DEPTH:], a_low[:, DEPTH:], *xs)
        if pair == pairs - 1:
            rest[...] = y[:, NX:]
        yh, yl = halves(y)
        for k in range(KERNELS):
            y_high[k, pair * BLOCK : (pair + 1) * BLOCK] = yh[k * BLOCK : (k + 1) * BLOCK]
            y_low[k, pair * BLOCK : (pair + 1) * BLOCK] = yl[k * BLOCK : (k + 1) * BLOCK]
    squares = []
    for k in range(KERNELS):
        z = dot3(y_high[k], y_low[k], h_high[k], h_low[k])
        for pair in range(pairs):
            part = z[pair * BLOCK : (pair + 1) * BLOCK]
            smoothed[k, pair] = part
            squared = row_squares(part)
            squares += [squared[:, :NX], squared[:, NX:]][: groups - 1 - 2 * pair]
    squares.append(jnp.zeros((KERNELS * GROUP, NX), F32))
    sums[...] = lane_sums(jnp.concatenate(squares, axis=0))


def tail_kernel(parity, edge, a_high, a_low, h_high, h_low, rest, main_sums, smoothed, sums):
    values = jnp.concatenate([edge[...], jnp.zeros((1, ROWS + 2 * RAD, NX), F32)], axis=0)
    border = border_rows(parity[0], values[:, :RAD], values[:, RAD + ROWS :])
    x = [part.reshape(BLOCK, NX) for part in (values[:, RAD : RAD + ROWS], border)]
    late = [slice(BLOCK, DEPTH), slice(DEPTH + BLOCK, 2 * DEPTH)]
    a = [jnp.concatenate([ref[:, part] for part in late], axis=1) for ref in (a_high, a_low)]
    yh, yl = halves(rest[...] + dot3(*a, *halves(jnp.concatenate(x, axis=0))))
    squares = [jnp.zeros((NX - KERNELS * GROUP, NX), F32)]
    for k in range(KERNELS):
        rows = slice(k * BLOCK, (k + 1) * BLOCK)
        z = dot3(yh[rows], yl[rows], h_high[k, :NX, :NX], h_low[k, :NX, :NX])
        smoothed[k] = z
        squares.append(row_squares(z))
    total = lane_sums(jnp.concatenate(squares, axis=0))
    low = jnp.broadcast_to(main_sums[0:1, :NX], sums.shape)
    high = jnp.broadcast_to(main_sums[0:1, NX:] + total[0:1], sums.shape)
    sums[...] = jnp.where(lax.broadcasted_iota(jnp.int32, sums.shape, 0) % 2 == 0, low, high)


def peak_kernel(cells, copies, widths, received, smoothed, last, peaks, scale):
    groups = 2 * smoothed.shape[1]
    per_kernel = (groups - 1) * GROUP
    total = jnp.sum(received[...].reshape(-1, 8, NX), axis=0)
    total = total[0:2] + total[2:4] + (total[4:6] + total[6:8])
    for h in (0, 1):
        index = h * NX + lax.broadcasted_iota(jnp.int32, (1, NX), 1)
        kernel = jnp.where(index < KERNELS * per_kernel, index // per_kernel, (index - KERNELS * per_kernel) // GROUP)
        width = jnp.full((1, NX), widths[0], jnp.int32)
        for k in range(1, KERNELS):
            width = jnp.where(kernel == k, widths[k], width)
        inverse = 1.0 / jnp.sqrt(total[h : h + 1] * (1.0 / cells) + width.astype(F32) * EPSILON)
        scale[h * NX : (h + 1) * NX, :] = jnp.broadcast_to(inverse, (NX, NX)).T
    for k in range(KERNELS):
        best = None
        for group in range(groups):
            for c in range(GROUP):
                rows = slice(c * ROWS, (c + 1) * ROWS)
                if group < groups - 1:
                    lanes = slice((group % 2) * NX, (group % 2 + 1) * NX)
                    at = k * per_kernel + group * GROUP + c
                    value = smoothed[k, group // 2, rows, lanes]
                else:
                    at = KERNELS * per_kernel + k * GROUP + c
                    value = last[k, rows]
                value = value * scale[at : at + 1]
                best = value if best is None else jnp.maximum(best, value)
        for i in range(copies):
            peaks[i, k] = best


def call(kernel, out_shape, in_specs, scratch=(), flops=0, moved=0):
    return pl.pallas_call(
        kernel,
        out_shape=out_shape,
        in_specs=in_specs,
        out_specs=jax.tree.map(lambda _: VMEM, out_shape),
        scratch_shapes=list(scratch),
        compiler_params=PARAMS,
        cost_estimate=pl.CostEstimate(flops=flops, bytes_accessed=moved, transcendentals=0),
    )


def body(planes, widths):
    tiles, blocks = lax.axis_size("tile"), lax.axis_size("fblk")
    shape = jax.ShapeDtypeStruct
    parity = jnp.reshape(lax.axis_index("tile") % 2, (1,)).astype(jnp.int32)
    own = lax.all_to_all(planes, "tile", split_axis=1, concat_axis=0, tiled=True)
    channels = own.shape[0]
    pairs = channels // (2 * GROUP)
    cells = ROWS * tiles * NX
    a_high, a_low = map(jnp.asarray, split(vertical_matrix()))
    h_high, h_low = map(jnp.asarray, split(horizontal_matrices()))
    a_shape = shape(a_high.shape, BF)
    a_high, a_low = call(mask_kernel, [a_shape, a_shape], [SMEM, VMEM, VMEM], moved=2**21)(widths, a_high, a_low)
    own, a_high, a_low = lax.optimization_barrier((own, a_high, a_low))

    odd = parity[0] == 1
    top, bottom = own[:, :RAD], own[:, ROWS - RAD :]
    inner = [(i + 1, i + 2) for i in range(0, tiles - 2, 2)]
    off = lax.ppermute(jnp.where(odd, bottom, top), "tile", inner + [(b, a) for a, b in inner])
    flip = lax.ppermute(jnp.where(odd, top, bottom), "tile", [(i, i ^ 1) for i in range(tiles)])
    first = slice(0, MAXW - 1)
    edge = jnp.concatenate([off[first], own[first], flip[first]], axis=1)
    edge = lax.ppermute(edge, "fblk", [(i + 1, i) for i in range(blocks - 1)])

    matrices = (a_high, a_low, h_high, h_low)
    rows_scratch = [pltpu.VMEM((channels + GROUP, ROWS, NX), BF)] * 2
    partial = call(
        own_kernel,
        shape((pairs, KERNELS * BLOCK, 2 * NX), F32),
        [VMEM] * 3,
        rows_scratch,
        flops=2**30,
        moved=2**22,
    )(own, a_high, a_low)
    smoothed, rest, sums = call(
        main_kernel,
        [
            shape((KERNELS, pairs, BLOCK, 2 * NX), F32),
            shape((KERNELS * BLOCK, NX), F32),
            shape((8, KERNELS * channels), F32),
        ],
        [SMEM] + [VMEM] * 7,
        rows_scratch + [pltpu.VMEM((KERNELS, pairs * BLOCK, 2 * NX), BF)] * 2,
        flops=2**31,
        moved=2**23,
    )(parity, off, flip, partial, *matrices)
    last, sums = call(
        tail_kernel,
        [shape((KERNELS, BLOCK, NX), F32), shape((2 * tiles, NX), F32)],
        [SMEM] + [VMEM] * 7,
        flops=2**29,
        moved=2**20,
    )(parity, edge, *matrices, rest, sums)
    received = lax.all_to_all(
        sums, "tile", split_axis=0, concat_axis=0, tiled=True, axis_index_groups=[list(range(tiles))[::-1]]
    )
    peaks = call(
        lambda *refs: peak_kernel(cells, blocks, *refs),
        shape((blocks, KERNELS, ROWS, NX), F32),
        [SMEM] + [VMEM] * 3,
        [pltpu.VMEM((KERNELS * channels, NX), F32)],
        moved=2**22,
    )(widths, received, smoothed, last)
    peaks = lax.all_to_all(
        peaks, "fblk", split_axis=0, concat_axis=0, tiled=True, axis_index_groups=[list(range(blocks))[::-1]]
    )
    return jnp.max(peaks, axis=0)


def solution(mesh):
    placed = (P(("fblk", "tile"), None, None), P())
    return jax.shard_map(body, mesh=mesh, in_specs=placed, out_specs=P(None, "tile", None), check_vma=False)
```

```python
import jax
import jax.numpy as jnp
import numpy as np
from jax import lax
from jax.experimental import pallas as pl
from jax.experimental.pallas import tpu as pltpu
from jax.sharding import PartitionSpec as P

KERNELS = 4
RAD = 8
MAXW = 8
SIGMAS = (1.0, 1.6, 2.3, 3.2)
EPSILON = 1e-06
ROWS = 16
GROUP = 8
NX = 128
BLOCK = GROUP * ROWS
DEPTH = 2 * GROUP * ROWS
BF = jnp.bfloat16
F32 = jnp.float32
VMEM = pl.BlockSpec(memory_space=pltpu.VMEM)
SMEM = pl.BlockSpec(memory_space=pltpu.SMEM)
PARAMS = pltpu.CompilerParams(vmem_limit_bytes=32 * 1024 * 1024)


def taps(sigma):
    offsets = np.arange(2 * RAD + 1) - RAD
    values = np.exp(-(offsets**2) / (2.0 * sigma * sigma))
    return values / values.sum()


def split(matrix):
    matrix = np.asarray(matrix, np.float32)
    high = matrix.astype(BF)
    return high, (matrix - high.astype(np.float32)).astype(BF)


def vertical_matrix():
    out = np.zeros((KERNELS, GROUP, ROWS, 2 * GROUP, ROWS + 2 * RAD))
    for k, sigma in enumerate(SIGMAS):
        weights = taps(sigma)
        for row in range(ROWS):
            for channel in range(GROUP):
                for offset in range(MAXW):
                    out[k, channel, row, channel + offset, row : row + 2 * RAD + 1] = weights
    own = out[..., RAD : RAD + ROWS]
    border = np.concatenate([out[..., :RAD], out[..., RAD + ROWS :]], axis=-1)
    return np.concatenate([x.reshape(KERNELS * BLOCK, DEPTH) for x in (own, border)], axis=1)


def horizontal_matrices():
    out = np.zeros((KERNELS, 2, NX, 2, NX))
    for k, sigma in enumerate(SIGMAS):
        weights = taps(sigma)
        for x in range(NX):
            for j in range(-RAD, RAD + 1):
                if 0 <= x + j < NX:
                    out[k, :, x + j, :, x] = weights[j + RAD] * np.eye(2)
    return out.reshape(KERNELS, 2 * NX, 2 * NX)


def halves(values):
    high = values.astype(BF)
    return high, (values - high.astype(F32)).astype(BF)


def dot(a, b):
    return jnp.dot(a, b, preferred_element_type=F32)


def dot3(a_high, a_low, b_high, b_low):
    return dot(a_high, b_high) + (dot(a_low, b_high) + dot(a_high, b_low))


def lane_sums(rows):
    ones = jnp.ones((8, NX), BF)
    parts = [
        lax.dot_general(ones, half, (((1,), (1,)), ((), ())), preferred_element_type=F32) for half in halves(rows)
    ]
    return parts[0] + parts[1]


def row_squares(values):
    return jnp.sum((values * values).reshape(GROUP, ROWS, values.shape[1]), axis=1)


def mask_kernel(widths, high_in, low_in, high, low):
    shape = (BLOCK, 2 * DEPTH)
    column = lax.broadcasted_iota(jnp.int32, shape, 1) % DEPTH
    offset = column // ROWS - lax.broadcasted_iota(jnp.int32, shape, 0) // ROWS
    for k in range(KERNELS):
        keep = jnp.where(offset < widths[k], 1.0, 0.0)
        rows = pl.ds(k * BLOCK, BLOCK)
        high[rows, :] = (high_in[rows, :].astype(F32) * keep).astype(BF)
        low[rows, :] = (low_in[rows, :].astype(F32) * keep).astype(BF)


def border_rows(parity, off, flip):
    even = parity == 0
    return jnp.concatenate([jnp.where(even, off, flip), jnp.where(even, flip, off)], axis=1)


def fill(values, high, low):
    channels = values.shape[0]
    high[0:channels], low[0:channels] = halves(values)
    high[channels:] = jnp.zeros((GROUP, ROWS, NX), BF)
    low[channels:] = jnp.zeros((GROUP, ROWS, NX), BF)


def side_by_side(ref, pair):
    first = 2 * pair * GROUP
    parts = [ref[first + s : first + s + 2 * GROUP].reshape(DEPTH, NX) for s in (0, GROUP)]
    return jnp.concatenate(parts, axis=1)


def own_kernel(own, a_high, a_low, partial, x_high, x_low):
    fill(own[...], x_high, x_low)
    for pair in range(partial.shape[0]):
        xs = side_by_side(x_high, pair), side_by_side(x_low, pair)
        partial[pair] = dot3(a_high[:, :DEPTH], a_low[:, :DEPTH], *xs)


def main_kernel(parity, off, flip, partial, a_high, a_low, h_high, h_low, smoothed, rest, sums, x_high, x_low, y_high, y_low):
    pairs = partial.shape[0]
    groups = 2 * pairs
    fill(border_rows(parity[0], off[...], flip[...]), x_high, x_low)
    for pair in range(pairs):
        xs = side_by_side(x_high, pair), side_by_side(x_low, pair)
        y = partial[pair] + dot3(a_high[:, DEPTH:], a_low[:, DEPTH:], *xs)
        if pair == pairs - 1:
            rest[...] = y[:, NX:]
        yh, yl = halves(y)
        for k in range(KERNELS):
            y_high[k, pair * BLOCK : (pair + 1) * BLOCK] = yh[k * BLOCK : (k + 1) * BLOCK]
            y_low[k, pair * BLOCK : (pair + 1) * BLOCK] = yl[k * BLOCK : (k + 1) * BLOCK]
    squares = []
    for k in range(KERNELS):
        z = dot3(y_high[k], y_low[k], h_high[k], h_low[k])
        for pair in range(pairs):
            part = z[pair * BLOCK : (pair + 1) * BLOCK]
            smoothed[k, pair] = part
            squared = row_squares(part)
            squares += [squared[:, :NX], squared[:, NX:]][: groups - 1 - 2 * pair]
    squares.append(jnp.zeros((KERNELS * GROUP, NX), F32))
    sums[...] = lane_sums(jnp.concatenate(squares, axis=0))


def tail_kernel(parity, edge_own, edge, a_high, a_low, h_high, h_low, rest, main_sums, smoothed, sums):
    border = border_rows(parity[0], edge[:, :RAD], edge[:, RAD:])
    zero = jnp.zeros((1, ROWS, NX), F32)
    x = [jnp.concatenate([part, zero], axis=0).reshape(BLOCK, NX) for part in (edge_own[...], border)]
    late = [slice(BLOCK, DEPTH), slice(DEPTH + BLOCK, 2 * DEPTH)]
    a = [jnp.concatenate([ref[:, part] for part in late], axis=1) for ref in (a_high, a_low)]
    yh, yl = halves(rest[...] + dot3(*a, *halves(jnp.concatenate(x, axis=0))))
    squares = [jnp.zeros((NX - KERNELS * GROUP, NX), F32)]
    for k in range(KERNELS):
        rows = slice(k * BLOCK, (k + 1) * BLOCK)
        z = dot3(yh[rows], yl[rows], h_high[k, :NX, :NX], h_low[k, :NX, :NX])
        smoothed[k] = z
        squares.append(row_squares(z))
    total = lane_sums(jnp.concatenate(squares, axis=0))
    low = jnp.broadcast_to(main_sums[0:1, :NX], sums.shape)
    high = jnp.broadcast_to(main_sums[0:1, NX:] + total[0:1], sums.shape)
    sums[...] = jnp.where(lax.broadcasted_iota(jnp.int32, sums.shape, 0) % 2 == 0, low, high)


def peak_kernel(cells, copies, widths, received, smoothed, last, peaks, scale):
    groups = 2 * smoothed.shape[1]
    per_kernel = (groups - 1) * GROUP
    total = jnp.sum(received[...].reshape(-1, 8, NX), axis=0)
    total = total[0:2] + total[2:4] + (total[4:6] + total[6:8])
    for h in (0, 1):
        index = h * NX + lax.broadcasted_iota(jnp.int32, (1, NX), 1)
        kernel = jnp.where(index < KERNELS * per_kernel, index // per_kernel, (index - KERNELS * per_kernel) // GROUP)
        width = jnp.full((1, NX), widths[0], jnp.int32)
        for k in range(1, KERNELS):
            width = jnp.where(kernel == k, widths[k], width)
        inverse = 1.0 / jnp.sqrt(total[h : h + 1] * (1.0 / cells) + width.astype(F32) * EPSILON)
        scale[h * NX : (h + 1) * NX, :] = jnp.broadcast_to(inverse, (NX, NX)).T
    for k in range(KERNELS):
        best = None
        for group in range(groups):
            for c in range(GROUP):
                rows = slice(c * ROWS, (c + 1) * ROWS)
                if group < groups - 1:
                    lanes = slice((group % 2) * NX, (group % 2 + 1) * NX)
                    at = k * per_kernel + group * GROUP + c
                    value = smoothed[k, group // 2, rows, lanes]
                else:
                    at = KERNELS * per_kernel + k * GROUP + c
                    value = last[k, rows]
                value = value * scale[at : at + 1]
                best = value if best is None else jnp.maximum(best, value)
        for i in range(copies):
            peaks[i, k] = best


def call(kernel, out_shape, in_specs, scratch=(), flops=0, moved=0):
    return pl.pallas_call(
        kernel,
        out_shape=out_shape,
        in_specs=in_specs,
        out_specs=jax.tree.map(lambda _: VMEM, out_shape),
        scratch_shapes=list(scratch),
        compiler_params=PARAMS,
        cost_estimate=pl.CostEstimate(flops=flops, bytes_accessed=moved, transcendentals=0),
    )


def body(planes, widths):
    tiles, blocks = lax.axis_size("tile"), lax.axis_size("fblk")
    shape = jax.ShapeDtypeStruct
    parity = jnp.reshape(lax.axis_index("tile") % 2, (1,)).astype(jnp.int32)
    own = lax.all_to_all(planes, "tile", split_axis=1, concat_axis=0, tiled=True)
    channels = own.shape[0]
    pairs = channels // (2 * GROUP)
    cells = ROWS * tiles * NX
    a_high, a_low = map(jnp.asarray, split(vertical_matrix()))
    h_high, h_low = map(jnp.asarray, split(horizontal_matrices()))
    a_shape = shape(a_high.shape, BF)
    a_high, a_low = call(mask_kernel, [a_shape, a_shape], [SMEM, VMEM, VMEM], moved=2**21)(widths, a_high, a_low)
    own, a_high, a_low = lax.optimization_barrier((own, a_high, a_low))

    odd = parity[0] == 1
    top, bottom = own[:, :RAD], own[:, ROWS - RAD :]
    inner = [(i + 1, i + 2) for i in range(0, tiles - 2, 2)]
    off = lax.ppermute(jnp.where(odd, bottom, top), "tile", inner + [(b, a) for a, b in inner])
    flip = lax.ppermute(jnp.where(odd, top, bottom), "tile", [(i, i ^ 1) for i in range(tiles)])
    first = slice(0, MAXW - 1)
    previous = [(i + 1, i) for i in range(blocks - 1)]
    edge_own = lax.ppermute(own[first], "fblk", previous)
    edge = jnp.concatenate([off[first], flip[first]], axis=1)
    edge = lax.ppermute(edge, "fblk", previous)

    matrices = (a_high, a_low, h_high, h_low)
    rows_scratch = [pltpu.VMEM((channels + GROUP, ROWS, NX), BF)] * 2
    partial = call(
        own_kernel,
        shape((pairs, KERNELS * BLOCK, 2 * NX), F32),
        [VMEM] * 3,
        rows_scratch,
        flops=2**30,
        moved=2**22,
    )(own, a_high, a_low)
    smoothed, rest, sums = call(
        main_kernel,
        [
            shape((KERNELS, pairs, BLOCK, 2 * NX), F32),
            shape((KERNELS * BLOCK, NX), F32),
            shape((8, KERNELS * channels), F32),
        ],
        [SMEM] + [VMEM] * 7,
        rows_scratch + [pltpu.VMEM((KERNELS, pairs * BLOCK, 2 * NX), BF)] * 2,
        flops=2**31,
        moved=2**23,
    )(parity, off, flip, partial, *matrices)
    last, sums = call(
        tail_kernel,
        [shape((KERNELS, BLOCK, NX), F32), shape((2 * tiles, NX), F32)],
        [SMEM] + [VMEM] * 8,
        flops=2**29,
        moved=2**20,
    )(parity, edge_own, edge, *matrices, rest, sums)
    received = lax.all_to_all(
        sums, "tile", split_axis=0, concat_axis=0, tiled=True, axis_index_groups=[list(range(tiles))[::-1]]
    )
    peaks = call(
        lambda *refs: peak_kernel(cells, blocks, *refs),
        shape((blocks, KERNELS, ROWS, NX), F32),
        [SMEM] + [VMEM] * 3,
        [pltpu.VMEM((KERNELS * channels, NX), F32)],
        moved=2**22,
    )(widths, received, smoothed, last)
    peaks = lax.all_to_all(
        peaks, "fblk", split_axis=0, concat_axis=0, tiled=True, axis_index_groups=[list(range(blocks))[::-1]]
    )
    return jnp.max(peaks, axis=0)


def solution(mesh):
    placed = (P(("fblk", "tile"), None, None), P())
    return jax.shard_map(body, mesh=mesh, in_specs=placed, out_specs=P(None, "tile", None), check_vma=False)
```

```python
import jax
import jax.numpy as jnp
import numpy as np
from jax import lax
from jax.experimental import pallas as pl
from jax.experimental.pallas import tpu as pltpu
from jax.sharding import PartitionSpec as P

KERNELS = 4
RAD = 8
MAXW = 8
SIGMAS = (1.0, 1.6, 2.3, 3.2)
EPSILON = 1e-06
ROWS = 16
GROUP = 8
NX = 128
BLOCK = GROUP * ROWS
DEPTH = 2 * GROUP * ROWS
BF = jnp.bfloat16
F32 = jnp.float32
VMEM = pl.BlockSpec(memory_space=pltpu.VMEM)
SMEM = pl.BlockSpec(memory_space=pltpu.SMEM)
PARAMS = pltpu.CompilerParams(vmem_limit_bytes=32 * 1024 * 1024)


def taps(sigma):
    offsets = np.arange(2 * RAD + 1) - RAD
    values = np.exp(-(offsets**2) / (2.0 * sigma * sigma))
    return values / values.sum()


def split(matrix):
    matrix = np.asarray(matrix, np.float32)
    high = matrix.astype(BF)
    return high, (matrix - high.astype(np.float32)).astype(BF)


def vertical_matrix():
    out = np.zeros((KERNELS, GROUP, ROWS, 2 * GROUP, ROWS + 2 * RAD))
    for k, sigma in enumerate(SIGMAS):
        weights = taps(sigma)
        for row in range(ROWS):
            for channel in range(GROUP):
                for offset in range(MAXW):
                    out[k, channel, row, channel + offset, row : row + 2 * RAD + 1] = weights
    own = out[..., RAD : RAD + ROWS]
    border = np.concatenate([out[..., :RAD], out[..., RAD + ROWS :]], axis=-1)
    return np.concatenate([x.reshape(KERNELS * BLOCK, DEPTH) for x in (own, border)], axis=1)


def horizontal_matrices():
    out = np.zeros((KERNELS, 2, NX, 2, NX))
    for k, sigma in enumerate(SIGMAS):
        weights = taps(sigma)
        for x in range(NX):
            for j in range(-RAD, RAD + 1):
                if 0 <= x + j < NX:
                    out[k, :, x + j, :, x] = weights[j + RAD] * np.eye(2)
    return out.reshape(KERNELS, 2 * NX, 2 * NX)


def halves(values):
    high = values.astype(BF)
    return high, (values - high.astype(F32)).astype(BF)


def dot(a, b):
    return jnp.dot(a, b, preferred_element_type=F32)


def dot3(a_high, a_low, b_high, b_low):
    return dot(a_high, b_high) + (dot(a_low, b_high) + dot(a_high, b_low))


def lane_sums(rows):
    ones = jnp.ones((8, NX), BF)
    parts = [
        lax.dot_general(ones, half, (((1,), (1,)), ((), ())), preferred_element_type=F32) for half in halves(rows)
    ]
    return parts[0] + parts[1]


def row_squares(values):
    return jnp.sum((values * values).reshape(GROUP, ROWS, values.shape[1]), axis=1)


def mask_kernel(per_kernel, widths, high_in, low_in, high, low, floor):
    index = lax.broadcasted_iota(jnp.int32, (2, NX), 0) * NX + lax.broadcasted_iota(jnp.int32, (2, NX), 1)
    kernel = jnp.where(index < KERNELS * per_kernel, index // per_kernel, (index - KERNELS * per_kernel) // GROUP)
    width = jnp.full((2, NX), widths[0], jnp.int32)
    for k in range(1, KERNELS):
        width = jnp.where(kernel == k, widths[k], width)
    floor[...] = width.astype(F32) * EPSILON
    shape = (BLOCK, 2 * DEPTH)
    column = lax.broadcasted_iota(jnp.int32, shape, 1) % DEPTH
    offset = column // ROWS - lax.broadcasted_iota(jnp.int32, shape, 0) // ROWS
    for k in range(KERNELS):
        keep = jnp.where(offset < widths[k], 1.0, 0.0)
        rows = pl.ds(k * BLOCK, BLOCK)
        high[rows, :] = (high_in[rows, :].astype(F32) * keep).astype(BF)
        low[rows, :] = (low_in[rows, :].astype(F32) * keep).astype(BF)


def border_rows(parity, off, flip):
    even = parity == 0
    return jnp.concatenate([jnp.where(even, off, flip), jnp.where(even, flip, off)], axis=1)


def fill(values, high, low):
    channels = values.shape[0]
    high[0:channels], low[0:channels] = halves(values)
    high[channels:] = jnp.zeros((GROUP, ROWS, NX), BF)
    low[channels:] = jnp.zeros((GROUP, ROWS, NX), BF)


def side_by_side(ref, pair):
    first = 2 * pair * GROUP
    parts = [ref[first + s : first + s + 2 * GROUP].reshape(DEPTH, NX) for s in (0, GROUP)]
    return jnp.concatenate(parts, axis=1)


def own_kernel(own, a_high, a_low, partial, x_high, x_low):
    fill(own[...], x_high, x_low)
    for pair in range(partial.shape[0]):
        xs = side_by_side(x_high, pair), side_by_side(x_low, pair)
        partial[pair] = dot3(a_high[:, :DEPTH], a_low[:, :DEPTH], *xs)


def main_kernel(parity, off, flip, partial, a_high, a_low, h_high, h_low, smoothed, rest, sums, x_high, x_low, y_high, y_low):
    pairs = partial.shape[0]
    groups = 2 * pairs
    fill(border_rows(parity[0], off[...], flip[...]), x_high, x_low)
    for pair in range(pairs):
        xs = side_by_side(x_high, pair), side_by_side(x_low, pair)
        y = partial[pair] + dot3(a_high[:, DEPTH:], a_low[:, DEPTH:], *xs)
        if pair == pairs - 1:
            rest[...] = y[:, NX:]
        yh, yl = halves(y)
        for k in range(KERNELS):
            y_high[k, pair * BLOCK : (pair + 1) * BLOCK] = yh[k * BLOCK : (k + 1) * BLOCK]
            y_low[k, pair * BLOCK : (pair + 1) * BLOCK] = yl[k * BLOCK : (k + 1) * BLOCK]
    squares = []
    for k in range(KERNELS):
        z = dot3(y_high[k], y_low[k], h_high[k], h_low[k])
        for pair in range(pairs):
            part = z[pair * BLOCK : (pair + 1) * BLOCK]
            smoothed[k, pair] = part
            squared = row_squares(part)
            squares += [squared[:, :NX], squared[:, NX:]][: groups - 1 - 2 * pair]
    squares.append(jnp.zeros((KERNELS * GROUP, NX), F32))
    sums[...] = lane_sums(jnp.concatenate(squares, axis=0))


def tail_kernel(parity, edge_own, edge, a_high, a_low, h_high, h_low, rest, main_sums, smoothed, sums):
    border = border_rows(parity[0], edge[:, :RAD], edge[:, RAD:])
    zero = jnp.zeros((1, ROWS, NX), F32)
    x = [jnp.concatenate([part, zero], axis=0).reshape(BLOCK, NX) for part in (edge_own[...], border)]
    late = [slice(BLOCK, DEPTH), slice(DEPTH + BLOCK, 2 * DEPTH)]
    a = [jnp.concatenate([ref[:, part] for part in late], axis=1) for ref in (a_high, a_low)]
    yh, yl = halves(rest[...] + dot3(*a, *halves(jnp.concatenate(x, axis=0))))
    squares = [jnp.zeros((NX - KERNELS * GROUP, NX), F32)]
    for k in range(KERNELS):
        rows = slice(k * BLOCK, (k + 1) * BLOCK)
        z = dot3(yh[rows], yl[rows], h_high[k, :NX, :NX], h_low[k, :NX, :NX])
        smoothed[k] = z
        squares.append(row_squares(z))
    total = lane_sums(jnp.concatenate(squares, axis=0))
    low = jnp.broadcast_to(main_sums[0:1, :NX], sums.shape)
    high = jnp.broadcast_to(main_sums[0:1, NX:] + total[0:1], sums.shape)
    sums[...] = jnp.where(lax.broadcasted_iota(jnp.int32, sums.shape, 0) % 2 == 0, low, high)


def peak_kernel(cells, copies, floor, received, smoothed, last, peaks, scale):
    groups = 2 * smoothed.shape[1]
    per_kernel = (groups - 1) * GROUP
    total = jnp.sum(received[...].reshape(-1, 8, NX), axis=0)
    total = total[0:2] + total[2:4] + (total[4:6] + total[6:8])
    inverse = 1.0 / jnp.sqrt(total * (1.0 / cells) + floor[...])
    for h in (0, 1):
        scale[h * NX : (h + 1) * NX, :] = jnp.broadcast_to(inverse[h : h + 1], (NX, NX)).T
    for k in range(KERNELS):
        best = None
        for group in range(groups):
            for c in range(GROUP):
                rows = slice(c * ROWS, (c + 1) * ROWS)
                if group < groups - 1:
                    lanes = slice((group % 2) * NX, (group % 2 + 1) * NX)
                    at = k * per_kernel + group * GROUP + c
                    value = smoothed[k, group // 2, rows, lanes]
                else:
                    at = KERNELS * per_kernel + k * GROUP + c
                    value = last[k, rows]
                value = value * scale[at : at + 1]
                best = value if best is None else jnp.maximum(best, value)
        for i in range(copies):
            peaks[i, k] = best


def call(kernel, out_shape, in_specs, scratch=(), flops=0, moved=0):
    return pl.pallas_call(
        kernel,
        out_shape=out_shape,
        in_specs=in_specs,
        out_specs=jax.tree.map(lambda _: VMEM, out_shape),
        scratch_shapes=list(scratch),
        compiler_params=PARAMS,
        cost_estimate=pl.CostEstimate(flops=flops, bytes_accessed=moved, transcendentals=0),
    )


def body(planes, widths):
    tiles, blocks = lax.axis_size("tile"), lax.axis_size("fblk")
    shape = jax.ShapeDtypeStruct
    parity = jnp.reshape(lax.axis_index("tile") % 2, (1,)).astype(jnp.int32)
    own = lax.all_to_all(planes, "tile", split_axis=1, concat_axis=0, tiled=True)
    channels = own.shape[0]
    pairs = channels // (2 * GROUP)
    cells = ROWS * tiles * NX
    a_high, a_low = map(jnp.asarray, split(vertical_matrix()))
    h_high, h_low = map(jnp.asarray, split(horizontal_matrices()))
    a_shape = shape(a_high.shape, BF)
    a_high, a_low, floor = call(
        lambda *refs: mask_kernel(channels - GROUP, *refs),
        [a_shape, a_shape, shape((2, NX), F32)],
        [SMEM, VMEM, VMEM],
        moved=2**21,
    )(widths, a_high, a_low)
    own, a_high, a_low = lax.optimization_barrier((own, a_high, a_low))

    odd = parity[0] == 1
    top, bottom = own[:, :RAD], own[:, ROWS - RAD :]
    inner = [(i + 1, i + 2) for i in range(0, tiles - 2, 2)]
    off = lax.ppermute(jnp.where(odd, bottom, top), "tile", inner + [(b, a) for a, b in inner])
    flip = lax.ppermute(jnp.where(odd, top, bottom), "tile", [(i, i ^ 1) for i in range(tiles)])
    first = slice(0, MAXW - 1)
    previous = [(i + 1, i) for i in range(blocks - 1)]
    edge_own = lax.ppermute(own[first], "fblk", previous)
    edge = jnp.concatenate([off[first], flip[first]], axis=1)
    edge = lax.ppermute(edge, "fblk", previous)

    matrices = (a_high, a_low, h_high, h_low)
    rows_scratch = [pltpu.VMEM((channels + GROUP, ROWS, NX), BF)] * 2
    partial = call(
        own_kernel,
        shape((pairs, KERNELS * BLOCK, 2 * NX), F32),
        [VMEM] * 3,
        rows_scratch,
        flops=2**30,
        moved=2**22,
    )(own, a_high, a_low)
    smoothed, rest, sums = call(
        main_kernel,
        [
            shape((KERNELS, pairs, BLOCK, 2 * NX), F32),
            shape((KERNELS * BLOCK, NX), F32),
            shape((8, KERNELS * channels), F32),
        ],
        [SMEM] + [VMEM] * 7,
        rows_scratch + [pltpu.VMEM((KERNELS, pairs * BLOCK, 2 * NX), BF)] * 2,
        flops=2**31,
        moved=2**23,
    )(parity, off, flip, partial, *matrices)
    last, sums = call(
        tail_kernel,
        [shape((KERNELS, BLOCK, NX), F32), shape((2 * tiles, NX), F32)],
        [SMEM] + [VMEM] * 8,
        flops=2**29,
        moved=2**20,
    )(parity, edge_own, edge, *matrices, rest, sums)
    received = lax.all_to_all(
        sums, "tile", split_axis=0, concat_axis=0, tiled=True, axis_index_groups=[[(3 * tiles // 4 - 1 - i) % tiles for i in range(tiles)]]
    )
    peaks = call(
        lambda *refs: peak_kernel(cells, blocks, *refs),
        shape((blocks, KERNELS, ROWS, NX), F32),
        [VMEM] * 4,
        [pltpu.VMEM((KERNELS * channels, NX), F32)],
        moved=2**22,
    )(floor, received, smoothed, last)
    peaks = lax.all_to_all(
        peaks, "fblk", split_axis=0, concat_axis=0, tiled=True, axis_index_groups=[list(range(blocks))[::-1]]
    )
    return jnp.max(peaks, axis=0)


def solution(mesh):
    placed = (P(("fblk", "tile"), None, None), P())
    return jax.shard_map(body, mesh=mesh, in_specs=placed, out_specs=P(None, "tile", None), check_vma=False)
```

```python
import jax
import jax.numpy as jnp
import numpy as np
from jax import lax
from jax.experimental import pallas as pl
from jax.experimental.pallas import tpu as pltpu
from jax.sharding import PartitionSpec as P

KERNELS = 4
RAD = 8
MAXW = 8
SIGMAS = (1.0, 1.6, 2.3, 3.2)
EPSILON = 1e-06
ROWS = 16
GROUP = 8
NX = 128
BLOCK = GROUP * ROWS
DEPTH = 2 * GROUP * ROWS
BF = jnp.bfloat16
F32 = jnp.float32
VMEM = pl.BlockSpec(memory_space=pltpu.VMEM)
SMEM = pl.BlockSpec(memory_space=pltpu.SMEM)
PARAMS = pltpu.CompilerParams(vmem_limit_bytes=32 * 1024 * 1024)


def taps(sigma):
    offsets = np.arange(2 * RAD + 1) - RAD
    values = np.exp(-(offsets**2) / (2.0 * sigma * sigma))
    return values / values.sum()


def split(matrix):
    matrix = np.asarray(matrix, np.float32)
    high = matrix.astype(BF)
    return high, (matrix - high.astype(np.float32)).astype(BF)


def vertical_matrix():
    out = np.zeros((KERNELS, GROUP, ROWS, 2 * GROUP, ROWS + 2 * RAD))
    for k, sigma in enumerate(SIGMAS):
        weights = taps(sigma)
        for row in range(ROWS):
            for channel in range(GROUP):
                for offset in range(MAXW):
                    out[k, channel, row, channel + offset, row : row + 2 * RAD + 1] = weights
    own = out[..., RAD : RAD + ROWS]
    border = np.concatenate([out[..., :RAD], out[..., RAD + ROWS :]], axis=-1)
    return np.concatenate([x.reshape(KERNELS * BLOCK, DEPTH) for x in (own, border)], axis=1)


def horizontal_matrices():
    out = np.zeros((KERNELS, 2, NX, 2, NX))
    for k, sigma in enumerate(SIGMAS):
        weights = taps(sigma)
        for x in range(NX):
            for j in range(-RAD, RAD + 1):
                if 0 <= x + j < NX:
                    out[k, :, x + j, :, x] = weights[j + RAD] * np.eye(2)
    return out.reshape(KERNELS, 2 * NX, 2 * NX)


def halves(values):
    high = values.astype(BF)
    return high, (values - high.astype(F32)).astype(BF)


def dot(a, b):
    return jnp.dot(a, b, preferred_element_type=F32)


def dot3(a_high, a_low, b_high, b_low):
    return dot(a_high, b_high) + (dot(a_low, b_high) + dot(a_high, b_low))


def lane_sums(rows):
    ones = jnp.ones((8, NX), BF)
    parts = [
        lax.dot_general(ones, half, (((1,), (1,)), ((), ())), preferred_element_type=F32) for half in halves(rows)
    ]
    return parts[0] + parts[1]


def row_squares(values):
    return jnp.sum((values * values).reshape(GROUP, ROWS, values.shape[1]), axis=1)


def mask_kernel(per_kernel, widths, high_in, low_in, high, low, floor):
    index = lax.broadcasted_iota(jnp.int32, (2, NX), 0) * NX + lax.broadcasted_iota(jnp.int32, (2, NX), 1)
    kernel = jnp.where(index < KERNELS * per_kernel, index // per_kernel, (index - KERNELS * per_kernel) // GROUP)
    width = jnp.full((2, NX), widths[0], jnp.int32)
    for k in range(1, KERNELS):
        width = jnp.where(kernel == k, widths[k], width)
    floor[...] = width.astype(F32) * EPSILON
    shape = (BLOCK, 2 * DEPTH)
    column = lax.broadcasted_iota(jnp.int32, shape, 1) % DEPTH
    offset = column // ROWS - lax.broadcasted_iota(jnp.int32, shape, 0) // ROWS
    for k in range(KERNELS):
        keep = jnp.where(offset < widths[k], 1.0, 0.0)
        rows = pl.ds(k * BLOCK, BLOCK)
        high[rows, :] = (high_in[rows, :].astype(F32) * keep).astype(BF)
        low[rows, :] = (low_in[rows, :].astype(F32) * keep).astype(BF)


def border_rows(parity, off, flip):
    even = parity == 0
    return jnp.concatenate([jnp.where(even, off, flip), jnp.where(even, flip, off)], axis=1)


def fill(values, high, low):
    channels = values.shape[0]
    high[0:channels], low[0:channels] = halves(values)
    high[channels:] = jnp.zeros((GROUP, ROWS, NX), BF)
    low[channels:] = jnp.zeros((GROUP, ROWS, NX), BF)


def side_by_side(ref, pair):
    first = 2 * pair * GROUP
    parts = [ref[first + s : first + s + 2 * GROUP].reshape(DEPTH, NX) for s in (0, GROUP)]
    return jnp.concatenate(parts, axis=1)


def own_kernel(own, a_high, a_low, partial, x_high, x_low):
    fill(own[...], x_high, x_low)
    for pair in range(partial.shape[0]):
        xs = side_by_side(x_high, pair), side_by_side(x_low, pair)
        partial[pair] = dot3(a_high[:, :DEPTH], a_low[:, :DEPTH], *xs)


def main_kernel(parity, off, flip, partial, a_high, a_low, h_high, h_low, smoothed, rest, sums, x_high, x_low, y_high, y_low):
    pairs = partial.shape[0]
    groups = 2 * pairs
    fill(border_rows(parity[0], off[...], flip[...]), x_high, x_low)
    for pair in range(pairs):
        xs = side_by_side(x_high, pair), side_by_side(x_low, pair)
        y = partial[pair] + dot3(a_high[:, DEPTH:], a_low[:, DEPTH:], *xs)
        if pair == pairs - 1:
            rest[...] = y[:, NX:]
        yh, yl = halves(y)
        for k in range(KERNELS):
            y_high[k, pair * BLOCK : (pair + 1) * BLOCK] = yh[k * BLOCK : (k + 1) * BLOCK]
            y_low[k, pair * BLOCK : (pair + 1) * BLOCK] = yl[k * BLOCK : (k + 1) * BLOCK]
    squares = []
    for k in range(KERNELS):
        z = dot3(y_high[k], y_low[k], h_high[k], h_low[k])
        for pair in range(pairs):
            part = z[pair * BLOCK : (pair + 1) * BLOCK]
            smoothed[k, pair] = part
            squared = row_squares(part)
            squares += [squared[:, :NX], squared[:, NX:]][: groups - 1 - 2 * pair]
    squares.append(jnp.zeros((KERNELS * GROUP, NX), F32))
    sums[...] = lane_sums(jnp.concatenate(squares, axis=0))


def tail_kernel(parity, edge_own, edge, a_high, a_low, h_high, h_low, rest, main_sums, smoothed, sums):
    border = border_rows(parity[0], edge[:, :RAD], edge[:, RAD:])
    zero = jnp.zeros((1, ROWS, NX), F32)
    x = [jnp.concatenate([part, zero], axis=0).reshape(BLOCK, NX) for part in (edge_own[...], border)]
    late = [slice(BLOCK, DEPTH), slice(DEPTH + BLOCK, 2 * DEPTH)]
    a = [jnp.concatenate([ref[:, part] for part in late], axis=1) for ref in (a_high, a_low)]
    yh, yl = halves(rest[...] + dot3(*a, *halves(jnp.concatenate(x, axis=0))))
    squares = [jnp.zeros((NX - KERNELS * GROUP, NX), F32)]
    for k in range(KERNELS):
        rows = slice(k * BLOCK, (k + 1) * BLOCK)
        z = dot3(yh[rows], yl[rows], h_high[k, :NX, :NX], h_low[k, :NX, :NX])
        smoothed[k] = z
        squares.append(row_squares(z))
    total = lane_sums(jnp.concatenate(squares, axis=0))
    odd = lax.broadcasted_iota(jnp.int32, (8, NX), 0) & 1
    both = jnp.where(odd == 0, main_sums[:, :NX], main_sums[:, NX:] + total)
    sums[...] = jnp.concatenate([both] * (sums.shape[0] // 8), axis=0)


def peak_kernel(cells, copies, floor, received, smoothed, last, peaks, scale):
    groups = 2 * smoothed.shape[1]
    per_kernel = (groups - 1) * GROUP
    total = jnp.sum(received[...].reshape(-1, 8, NX), axis=0)
    total = total[0:2] + total[2:4] + (total[4:6] + total[6:8])
    inverse = 1.0 / jnp.sqrt(total * (1.0 / cells) + floor[...])
    for h in (0, 1):
        scale[h * NX : (h + 1) * NX, :] = jnp.broadcast_to(inverse[h : h + 1], (NX, NX)).T
    for k in range(KERNELS):
        best = None
        for group in range(groups):
            for c in range(GROUP):
                rows = slice(c * ROWS, (c + 1) * ROWS)
                if group < groups - 1:
                    lanes = slice((group % 2) * NX, (group % 2 + 1) * NX)
                    at = k * per_kernel + group * GROUP + c
                    value = smoothed[k, group // 2, rows, lanes]
                else:
                    at = KERNELS * per_kernel + k * GROUP + c
                    value = last[k, rows]
                value = value * scale[at : at + 1]
                best = value if best is None else jnp.maximum(best, value)
        for i in range(copies):
            peaks[i, k] = best


def call(kernel, out_shape, in_specs, scratch=(), flops=0, moved=0):
    return pl.pallas_call(
        kernel,
        out_shape=out_shape,
        in_specs=in_specs,
        out_specs=jax.tree.map(lambda _: VMEM, out_shape),
        scratch_shapes=list(scratch),
        compiler_params=PARAMS,
        cost_estimate=pl.CostEstimate(flops=flops, bytes_accessed=moved, transcendentals=0),
    )


def body(planes, widths):
    tiles, blocks = lax.axis_size("tile"), lax.axis_size("fblk")
    shape = jax.ShapeDtypeStruct
    parity = jnp.reshape(lax.axis_index("tile") % 2, (1,)).astype(jnp.int32)
    own = lax.all_to_all(planes, "tile", split_axis=1, concat_axis=0, tiled=True)
    channels = own.shape[0]
    pairs = channels // (2 * GROUP)
    cells = ROWS * tiles * NX
    a_high, a_low = map(jnp.asarray, split(vertical_matrix()))
    h_high, h_low = map(jnp.asarray, split(horizontal_matrices()))
    a_shape = shape(a_high.shape, BF)
    a_high, a_low, floor = call(
        lambda *refs: mask_kernel(channels - GROUP, *refs),
        [a_shape, a_shape, shape((2, NX), F32)],
        [SMEM, VMEM, VMEM],
        moved=2**21,
    )(widths, a_high, a_low)
    own, a_high, a_low = lax.optimization_barrier((own, a_high, a_low))

    odd = parity[0] == 1
    top, bottom = own[:, :RAD], own[:, ROWS - RAD :]
    inner = [(i + 1, i + 2) for i in range(0, tiles - 2, 2)]
    off = lax.ppermute(jnp.where(odd, bottom, top), "tile", inner + [(b, a) for a, b in inner])
    flip = lax.ppermute(jnp.where(odd, top, bottom), "tile", [(i, i ^ 1) for i in range(tiles)])
    first = slice(0, MAXW - 1)
    previous = [(i + 1, i) for i in range(blocks - 1)]
    edge_own = lax.ppermute(own[first], "fblk", previous)
    edge = jnp.concatenate([off[first], flip[first]], axis=1)
    edge = lax.ppermute(edge, "fblk", previous)

    matrices = (a_high, a_low, h_high, h_low)
    rows_scratch = [pltpu.VMEM((channels + GROUP, ROWS, NX), BF)] * 2
    partial = call(
        own_kernel,
        shape((pairs, KERNELS * BLOCK, 2 * NX), F32),
        [VMEM] * 3,
        rows_scratch,
        flops=2**30,
        moved=2**22,
    )(own, a_high, a_low)
    smoothed, rest, sums = call(
        main_kernel,
        [
            shape((KERNELS, pairs, BLOCK, 2 * NX), F32),
            shape((KERNELS * BLOCK, NX), F32),
            shape((8, KERNELS * channels), F32),
        ],
        [SMEM] + [VMEM] * 7,
        rows_scratch + [pltpu.VMEM((KERNELS, pairs * BLOCK, 2 * NX), BF)] * 2,
        flops=2**31,
        moved=2**23,
    )(parity, off, flip, partial, *matrices)
    last, sums = call(
        tail_kernel,
        [shape((KERNELS, BLOCK, NX), F32), shape((2 * tiles, NX), F32)],
        [SMEM] + [VMEM] * 8,
        flops=2**29,
        moved=2**20,
    )(parity, edge_own, edge, *matrices, rest, sums)
    received = lax.all_to_all(
        sums, "tile", split_axis=0, concat_axis=0, tiled=True, axis_index_groups=[[(3 * tiles // 4 - 1 - i) % tiles for i in range(tiles)]]
    )
    peaks = call(
        lambda *refs: peak_kernel(cells, blocks, *refs),
        shape((blocks, KERNELS, ROWS, NX), F32),
        [VMEM] * 4,
        [pltpu.VMEM((KERNELS * channels, NX), F32)],
        moved=2**22,
    )(floor, received, smoothed, last)
    peaks = lax.all_to_all(
        peaks, "fblk", split_axis=0, concat_axis=0, tiled=True, axis_index_groups=[list(range(blocks))[::-1]]
    )
    return jnp.max(peaks, axis=0)


def solution(mesh):
    placed = (P(("fblk", "tile"), None, None), P())
    return jax.shard_map(body, mesh=mesh, in_specs=placed, out_specs=P(None, "tile", None), check_vma=False)
```

```python
import jax
import jax.numpy as jnp
import numpy as np
from jax import lax
from jax.experimental import pallas as pl
from jax.experimental.pallas import tpu as pltpu
from jax.sharding import PartitionSpec as P

KERNELS = 4
RAD = 8
MAXW = 8
SIGMAS = (1.0, 1.6, 2.3, 3.2)
EPSILON = 1e-06
ROWS = 16
GROUP = 8
NX = 128
BLOCK = GROUP * ROWS
DEPTH = 2 * GROUP * ROWS
BF = jnp.bfloat16
F32 = jnp.float32
VMEM = pl.BlockSpec(memory_space=pltpu.VMEM)
SMEM = pl.BlockSpec(memory_space=pltpu.SMEM)
PARAMS = pltpu.CompilerParams(vmem_limit_bytes=32 * 1024 * 1024)


def taps(sigma):
    offsets = np.arange(2 * RAD + 1) - RAD
    values = np.exp(-(offsets**2) / (2.0 * sigma * sigma))
    return values / values.sum()


def split(matrix):
    matrix = np.asarray(matrix, np.float32)
    high = matrix.astype(BF)
    return high, (matrix - high.astype(np.float32)).astype(BF)


def vertical_matrix():
    out = np.zeros((KERNELS, GROUP, ROWS, 2 * GROUP, ROWS + 2 * RAD))
    for k, sigma in enumerate(SIGMAS):
        weights = taps(sigma)
        for row in range(ROWS):
            for channel in range(GROUP):
                for offset in range(MAXW):
                    out[k, channel, row, channel + offset, row : row + 2 * RAD + 1] = weights
    own = out[..., RAD : RAD + ROWS]
    border = np.concatenate([out[..., :RAD], out[..., RAD + ROWS :]], axis=-1)
    return np.concatenate([x.reshape(KERNELS * BLOCK, DEPTH) for x in (own, border)], axis=1)


def horizontal_matrices():
    out = np.zeros((KERNELS, 2, NX, 2, NX))
    for k, sigma in enumerate(SIGMAS):
        weights = taps(sigma)
        for x in range(NX):
            for j in range(-RAD, RAD + 1):
                if 0 <= x + j < NX:
                    out[k, :, x + j, :, x] = weights[j + RAD] * np.eye(2)
    return out.reshape(KERNELS, 2 * NX, 2 * NX)


def halves(values):
    high = values.astype(BF)
    return high, (values - high.astype(F32)).astype(BF)


def dot(a, b):
    return jnp.dot(a, b, preferred_element_type=F32)


def dot3(a_high, a_low, b_high, b_low):
    return dot(a_high, b_high) + (dot(a_low, b_high) + dot(a_high, b_low))


def lane_sums(rows):
    ones = jnp.ones((8, NX), BF)
    parts = [
        lax.dot_general(ones, half, (((1,), (1,)), ((), ())), preferred_element_type=F32) for half in halves(rows)
    ]
    return parts[0] + parts[1]


def row_squares(values):
    return jnp.sum((values * values).reshape(GROUP, ROWS, values.shape[1]), axis=1)


def mask_kernel(per_kernel, widths, high_in, low_in, high, low, floor):
    index = lax.broadcasted_iota(jnp.int32, (2, NX), 0) * NX + lax.broadcasted_iota(jnp.int32, (2, NX), 1)
    kernel = jnp.where(index < KERNELS * per_kernel, index // per_kernel, (index - KERNELS * per_kernel) // GROUP)
    width = jnp.full((2, NX), widths[0], jnp.int32)
    for k in range(1, KERNELS):
        width = jnp.where(kernel == k, widths[k], width)
    floor[...] = width.astype(F32) * EPSILON
    shape = (BLOCK, 2 * DEPTH)
    column = lax.broadcasted_iota(jnp.int32, shape, 1) % DEPTH
    offset = column // ROWS - lax.broadcasted_iota(jnp.int32, shape, 0) // ROWS
    for k in range(KERNELS):
        keep = jnp.where(offset < widths[k], 1.0, 0.0)
        rows = pl.ds(k * BLOCK, BLOCK)
        high[rows, :] = (high_in[rows, :].astype(F32) * keep).astype(BF)
        low[rows, :] = (low_in[rows, :].astype(F32) * keep).astype(BF)


def border_rows(parity, off, flip):
    even = parity == 0
    return jnp.concatenate([jnp.where(even, off, flip), jnp.where(even, flip, off)], axis=1)


def fill(values, high, low):
    channels = values.shape[0]
    high[0:channels], low[0:channels] = halves(values)
    high[channels:] = jnp.zeros((GROUP, ROWS, NX), BF)
    low[channels:] = jnp.zeros((GROUP, ROWS, NX), BF)


def side_by_side(ref, pair):
    first = 2 * pair * GROUP
    parts = [ref[first + s : first + s + 2 * GROUP].reshape(DEPTH, NX) for s in (0, GROUP)]
    return jnp.concatenate(parts, axis=1)


def own_kernel(own, a_high, a_low, partial, x_high, x_low):
    fill(own[...], x_high, x_low)
    for pair in range(partial.shape[0]):
        xs = side_by_side(x_high, pair), side_by_side(x_low, pair)
        partial[pair] = dot3(a_high[:, :DEPTH], a_low[:, :DEPTH], *xs)


def main_kernel(parity, off, flip, partial, a_high, a_low, h_high, h_low, smoothed, rest, sums, x_high, x_low, y_high, y_low):
    pairs = partial.shape[0]
    groups = 2 * pairs
    fill(border_rows(parity[0], off[...], flip[...]), x_high, x_low)
    for pair in range(pairs):
        xs = side_by_side(x_high, pair), side_by_side(x_low, pair)
        y = partial[pair] + dot3(a_high[:, DEPTH:], a_low[:, DEPTH:], *xs)
        if pair == pairs - 1:
            rest[...] = y[:, NX:]
        yh, yl = halves(y)
        for k in range(KERNELS):
            y_high[k, pair * BLOCK : (pair + 1) * BLOCK] = yh[k * BLOCK : (k + 1) * BLOCK]
            y_low[k, pair * BLOCK : (pair + 1) * BLOCK] = yl[k * BLOCK : (k + 1) * BLOCK]
    squares = []
    for k in range(KERNELS):
        z = dot3(y_high[k], y_low[k], h_high[k], h_low[k])
        for pair in range(pairs):
            part = z[pair * BLOCK : (pair + 1) * BLOCK]
            smoothed[k, pair] = part
            squared = row_squares(part)
            squares += [squared[:, :NX], squared[:, NX:]][: groups - 1 - 2 * pair]
    squares.append(jnp.zeros((KERNELS * GROUP, NX), F32))
    sums[...] = lane_sums(jnp.concatenate(squares, axis=0))


def tail_kernel(parity, edge_own, edge, a_high, a_low, h_high, h_low, rest, main_sums, smoothed, sums):
    border = border_rows(parity[0], edge[:, :RAD], edge[:, RAD:])
    zero = jnp.zeros((1, ROWS, NX), F32)
    x = [jnp.concatenate([part, zero], axis=0).reshape(BLOCK, NX) for part in (edge_own[...], border)]
    late = [slice(BLOCK, DEPTH), slice(DEPTH + BLOCK, 2 * DEPTH)]
    a = [jnp.concatenate([ref[:, part] for part in late], axis=1) for ref in (a_high, a_low)]
    yh, yl = halves(rest[...] + dot3(*a, *halves(jnp.concatenate(x, axis=0))))
    squares = [jnp.zeros((NX - KERNELS * GROUP, NX), F32)]
    for k in range(KERNELS):
        rows = slice(k * BLOCK, (k + 1) * BLOCK)
        both = dot(jnp.concatenate([yh[rows], yl[rows]], axis=1), h_high[k])
        z = both[:, :NX] + (both[:, NX:] + dot(yh[rows], h_low[k, :NX, :NX]))
        smoothed[k] = z
        squares.append(row_squares(z))
    total = lane_sums(jnp.concatenate(squares, axis=0))
    odd = lax.broadcasted_iota(jnp.int32, (8, NX), 0) & 1
    both = jnp.where(odd == 0, main_sums[:, :NX], main_sums[:, NX:] + total)
    sums[...] = jnp.concatenate([both] * (sums.shape[0] // 8), axis=0)


def peak_kernel(cells, copies, floor, received, smoothed, last, peaks, scale):
    groups = 2 * smoothed.shape[1]
    per_kernel = (groups - 1) * GROUP
    total = jnp.sum(received[...].reshape(-1, 8, NX), axis=0)
    total = total[0:2] + total[2:4] + (total[4:6] + total[6:8])
    inverse = 1.0 / jnp.sqrt(total * (1.0 / cells) + floor[...])
    for h in (0, 1):
        scale[h * NX : (h + 1) * NX, :] = jnp.broadcast_to(inverse[h : h + 1], (NX, NX)).T
    for k in range(KERNELS):
        best = None
        for group in range(groups):
            for c in range(GROUP):
                rows = slice(c * ROWS, (c + 1) * ROWS)
                if group < groups - 1:
                    lanes = slice((group % 2) * NX, (group % 2 + 1) * NX)
                    at = k * per_kernel + group * GROUP + c
                    value = smoothed[k, group // 2, rows, lanes]
                else:
                    at = KERNELS * per_kernel + k * GROUP + c
                    value = last[k, rows]
                value = value * scale[at : at + 1]
                best = value if best is None else jnp.maximum(best, value)
        for i in range(copies):
            peaks[i, k] = best


def call(kernel, out_shape, in_specs, scratch=(), flops=0, moved=0):
    return pl.pallas_call(
        kernel,
        out_shape=out_shape,
        in_specs=in_specs,
        out_specs=jax.tree.map(lambda _: VMEM, out_shape),
        scratch_shapes=list(scratch),
        compiler_params=PARAMS,
        cost_estimate=pl.CostEstimate(flops=flops, bytes_accessed=moved, transcendentals=0),
    )


def body(planes, widths):
    tiles, blocks = lax.axis_size("tile"), lax.axis_size("fblk")
    shape = jax.ShapeDtypeStruct
    parity = jnp.reshape(lax.axis_index("tile") % 2, (1,)).astype(jnp.int32)
    own = lax.all_to_all(planes, "tile", split_axis=1, concat_axis=0, tiled=True)
    channels = own.shape[0]
    pairs = channels // (2 * GROUP)
    cells = ROWS * tiles * NX
    a_high, a_low = map(jnp.asarray, split(vertical_matrix()))
    h_high, h_low = map(jnp.asarray, split(horizontal_matrices()))
    a_shape = shape(a_high.shape, BF)
    a_high, a_low, floor = call(
        lambda *refs: mask_kernel(channels - GROUP, *refs),
        [a_shape, a_shape, shape((2, NX), F32)],
        [SMEM, VMEM, VMEM],
        moved=2**21,
    )(widths, a_high, a_low)
    own, a_high, a_low = lax.optimization_barrier((own, a_high, a_low))

    odd = parity[0] == 1
    top, bottom = own[:, :RAD], own[:, ROWS - RAD :]
    inner = [(i + 1, i + 2) for i in range(0, tiles - 2, 2)]
    off = lax.ppermute(jnp.where(odd, bottom, top), "tile", inner + [(b, a) for a, b in inner])
    flip = lax.ppermute(jnp.where(odd, top, bottom), "tile", [(i, i ^ 1) for i in range(tiles)])
    first = slice(0, MAXW - 1)
    previous = [(i + 1, i) for i in range(blocks - 1)]
    edge_own = lax.ppermute(own[first], "fblk", previous)
    edge = jnp.concatenate([off[first], flip[first]], axis=1)
    edge = lax.ppermute(edge, "fblk", previous)

    matrices = (a_high, a_low, h_high, h_low)
    rows_scratch = [pltpu.VMEM((channels + GROUP, ROWS, NX), BF)] * 2
    partial = call(
        own_kernel,
        shape((pairs, KERNELS * BLOCK, 2 * NX), F32),
        [VMEM] * 3,
        rows_scratch,
        flops=2**30,
        moved=2**22,
    )(own, a_high, a_low)
    smoothed, rest, sums = call(
        main_kernel,
        [
            shape((KERNELS, pairs, BLOCK, 2 * NX), F32),
            shape((KERNELS * BLOCK, NX), F32),
            shape((8, KERNELS * channels), F32),
        ],
        [SMEM] + [VMEM] * 7,
        rows_scratch + [pltpu.VMEM((KERNELS, pairs * BLOCK, 2 * NX), BF)] * 2,
        flops=2**31,
        moved=2**23,
    )(parity, off, flip, partial, *matrices)
    last, sums = call(
        tail_kernel,
        [shape((KERNELS, BLOCK, NX), F32), shape((2 * tiles, NX), F32)],
        [SMEM] + [VMEM] * 8,
        flops=2**29,
        moved=2**20,
    )(parity, edge_own, edge, *matrices, rest, sums)
    received = lax.all_to_all(
        sums, "tile", split_axis=0, concat_axis=0, tiled=True, axis_index_groups=[[(3 * tiles // 4 - 1 - i) % tiles for i in range(tiles)]]
    )
    peaks = call(
        lambda *refs: peak_kernel(cells, blocks, *refs),
        shape((blocks, KERNELS, ROWS, NX), F32),
        [VMEM] * 4,
        [pltpu.VMEM((KERNELS * channels, NX), F32)],
        moved=2**22,
    )(floor, received, smoothed, last)
    peaks = lax.all_to_all(
        peaks, "fblk", split_axis=0, concat_axis=0, tiled=True, axis_index_groups=[list(range(blocks))[::-1]]
    )
    return jnp.max(peaks, axis=0)


def solution(mesh):
    placed = (P(("fblk", "tile"), None, None), P())
    return jax.shard_map(body, mesh=mesh, in_specs=placed, out_specs=P(None, "tile", None), check_vma=False)
```
